768 devices in a mesh: dom: 96 (over z, x, core), sub: 8 (over y).
Axes of the slice: x: 4, y: 8, z: 12, core: 2. Of those that a mesh axis runs over, the one named last changes fastest.
Arguments:
- feats: bfloat16 [1572864, 128], P(('dom', 'sub')), may hold values from -6 to 6
- stale: bfloat16 [1572864, 128], P(('dom', 'sub')), may hold values from -6 to 6
- weight: bfloat16 [128, 128], replicated, may hold values from -0.5 to 0.5
- cotangent: bfloat16 [1572864, 128], P(('dom', 'sub')), may hold values from -6 to 6
- send_sub: int32 [6144, 64], P(('dom', 'sub')), may hold values from 0 to 2047
- send_dom: int32 [73728, 2], P(('dom', 'sub')), may hold values from 0 to 2047
- tile_index: int32 [768, 2, 48], P(('dom', 'sub')), may hold values from 0 to 21, as said below
- tile_count: int32 [768], P(('dom', 'sub')), may hold values from 22 to 48
- tile_values: bfloat16 [36864, 128, 128], P(('dom', 'sub')), may hold values from -0.3125 to 0.3125
Outputs:
- hidden_out: bfloat16 [1572864, 128], P(('dom', 'sub'))
- weight_grad: float32 [128, 128], replicated
- feat_grad: bfloat16 [1572864, 128], P(('dom', 'sub'))
The draws below stay inside these ranges and needn't reach their ends.
Inputs may be any that keep to these rules, and one draw needn't show every extreme that they name: `tile_index`: slots 6 to 21 have row blocks 0 to 15 in order and column blocks 0 to 15 in order; slot t < 6 has column block 16 + t.
All inputs are finite; a program needn't handle non-finite values.
Results may differ from the reference program's by a relative error of at most 0.007.
Values may be sent and summed in bfloat16 or wider, within the bound.
A program may use at most 32 MiB of HBM per device.

```python
import jax
import jax.numpy as jnp
from jax import lax

F = 128
HID = 128
NODES_DEV = 2048
TILE = 128
TILES = 48
SS = 64
SD = 2
NODES = 1572864
RB = 16
NH = 6
CB = 22
MINC = 22
N_DOM = 96
N_SUB = 8
DEVICES = 768


def draw_tile_index(key, part):
    key = jax.random.fold_in(key, 11)
    first_key, second_key = jax.random.split(key, 2)
    slot_ids = jnp.arange(TILES, dtype=jnp.int32)[None, :]
    rand_rows = jax.random.randint(first_key, (DEVICES, TILES), 0, RB)
    rand_cols = jax.random.randint(second_key, (DEVICES, TILES), 0, CB)
    row_ids = jnp.where((slot_ids >= NH) & (slot_ids < NH + RB), slot_ids - NH, rand_rows)
    col_ids = jnp.where(slot_ids < NH, RB + slot_ids, rand_cols)
    col_ids = jnp.where((slot_ids >= NH) & (slot_ids < NH + RB), slot_ids - NH, col_ids)
    return jnp.stack([row_ids, col_ids], axis=1).astype(jnp.int32)


def draw_tile_count(key, part):
    key = jax.random.fold_in(key, 23)
    first_key, second_key, third_key = jax.random.split(key, 3)
    spread_range = TILES - MINC
    first_draw = jax.random.randint(first_key, (DEVICES,), 0, spread_range + 1)
    second_draw = jax.random.randint(second_key, (DEVICES,), 0, spread_range + 1)
    counts_all = MINC + first_draw * second_draw // spread_range
    busiest = jax.random.randint(third_key, (), 0, DEVICES)
    device_ids = jnp.arange(DEVICES, dtype=jnp.int32)
    counts_all = jnp.where(device_ids == busiest, TILES, counts_all)
    counts_all = jnp.where(device_ids == (busiest + 1) % DEVICES, MINC, counts_all)
    return counts_all.astype(jnp.int32)


def set_ends(result, rng, least, high):
    shape = result.shape
    index_at = [jax.random.randint(jax.random.fold_in(rng, axis), (), 0, shape[axis]) for axis in range(len(shape))]
    result = result.at[tuple(index_at)].set(least)
    longest = shape.index(max(shape))
    index_at[longest] = (index_at[longest] + 1) % shape[longest]
    return result.at[tuple(index_at)].set(high)


def shard_levels(rng, dims, pieces, low, high):
    factor_of, own = 1.0, jax.random.fold_in(rng, 6)
    for axis_at, blocks in pieces:
        heights = jnp.exp(jax.random.uniform(jax.random.fold_in(own, axis_at), (blocks,), jnp.float32, low / len(pieces), high / len(pieces)))
        factor_of = factor_of * jnp.repeat(heights, dims[axis_at] // blocks).reshape([-1 if axis == axis_at else 1 for axis in range(len(dims))])
    return factor_of


def noise(own_key, shape, deviation, most, pieces=(), kind=jnp.bfloat16):
    drawn = jax.random.normal(own_key, shape, jnp.float32) * deviation
    if len(pieces) > 0:
        drawn = shard_levels(own_key, shape, pieces, -0.22, 0.18) * drawn
    return jnp.clip(drawn, min=-most, max=most).astype(kind)


def setup_inputs(seed: int = 0) -> dict:
    seeds = jax.random.split(jax.random.key(seed), 10)
    return {
        "feats": noise(seeds[0], (NODES, F), 1.0, 6.0, ((0, 768),)),
        "stale": noise(seeds[1], (NODES, F), 1.0, 6.0, ((0, 768),)),
        "weight": noise(seeds[2], (F, HID), F ** -0.5, 0.5),
        "cotangent": noise(seeds[3], (NODES, HID), 1.0, 6.0, ((0, 768),)),
        "send_sub": set_ends(jax.random.randint(seeds[4], (DEVICES * N_SUB, SS), 0, NODES_DEV), jax.random.fold_in(seeds[4], 1), 0, NODES_DEV - 1).astype(jnp.int32),
        "send_dom": set_ends(jax.random.randint(seeds[5], (DEVICES * N_DOM, SD), 0, NODES_DEV), jax.random.fold_in(seeds[5], 1), 0, NODES_DEV - 1).astype(jnp.int32),
        "tile_index": draw_tile_index(jax.random.fold_in(seeds[9], 71), 0),
        "tile_count": draw_tile_count(jax.random.fold_in(seeds[9], 71), 0),
        "tile_values": noise(seeds[8], (DEVICES * TILES, TILE, TILE), (TILE * TILES // RB) ** -0.5, 0.3125, ((0, 768),)),
    }


def local_pass(packed, weight):
    own_rows, halo_sub, halo_dom, grad_out, tile_index, tile_count, tile_values = packed
    columns = jnp.concatenate([own_rows, halo_sub.reshape(-1, F), halo_dom.reshape(-1, F)], axis=0)
    padding = jnp.zeros((CB * TILE - columns.shape[0], F), jnp.bfloat16)
    blocks = jnp.concatenate([columns, padding], axis=0).reshape(CB, TILE, F)
    live_mask = (jnp.arange(TILES) < tile_count)[:, None, None]
    masked = jnp.where(live_mask, tile_values, jnp.zeros_like(tile_values)).astype(jnp.float32)
    picked = blocks[tile_index[1]].astype(jnp.float32)
    products = jnp.einsum('tij,tjf->tif', masked, picked)
    row_onehot = (tile_index[0][None, :] == jnp.arange(RB)[:, None]).astype(jnp.float32)
    summed = jnp.einsum('rt,tif->rif', row_onehot, products, precision=lax.Precision.HIGHEST)
    aggregated = summed.reshape(NODES_DEV, F).astype(jnp.bfloat16)
    pre_act = jnp.dot(aggregated, weight, preferred_element_type=jnp.float32)
    hidden_rows = jax.nn.silu(pre_act).astype(jnp.bfloat16)
    gate_sig = jax.nn.sigmoid(pre_act)
    grad_z = (grad_out.astype(jnp.float32) * gate_sig * (1.0 + pre_act * (1.0 - gate_sig))).astype(jnp.bfloat16)
    weight_part = jnp.dot(aggregated.T, grad_z, preferred_element_type=jnp.float32)
    grad_agg = jnp.dot(grad_z, weight.T, preferred_element_type=jnp.float32).astype(jnp.bfloat16)
    grad_blocks = grad_agg.reshape(RB, TILE, F)[tile_index[0]].astype(jnp.float32)
    back_terms = jnp.einsum('tji,tjf->tif', masked, grad_blocks)
    col_onehot = (tile_index[1][None, :] == jnp.arange(CB)[:, None]).astype(jnp.float32)
    grad_columns = jnp.einsum('ct,tif->cif', col_onehot, back_terms, precision=lax.Precision.HIGHEST).reshape(CB * TILE, F)
    halo_total = N_SUB * SS + N_DOM * SD
    return (hidden_rows, weight_part, grad_columns[:NODES_DEV], grad_columns[NODES_DEV:NODES_DEV + halo_total])

def pick_rows(rows_of, lists):
    return rows_of[lists]

def reference(feats, stale, weight, cotangent, send_sub, send_dom, tile_index, tile_count, tile_values):
    stale_dev = stale.reshape(N_DOM, N_SUB, NODES_DEV, F)
    sub_lists = send_sub.reshape(N_DOM, N_SUB, N_SUB, SS)
    dom_lists = send_dom.reshape(N_DOM, N_SUB, N_DOM, SD)
    picked_sub = jax.vmap(jax.vmap(pick_rows))(stale_dev, sub_lists)
    halo_sub = picked_sub.transpose(0, 2, 1, 3, 4).reshape(DEVICES, N_SUB, SS, F)
    picked_dom = jax.vmap(jax.vmap(pick_rows))(stale_dev, dom_lists)
    halo_dom = picked_dom.transpose(2, 1, 0, 3, 4).reshape(DEVICES, N_DOM, SD, F)
    own_rows = feats.reshape(DEVICES, NODES_DEV, F)
    grad_out = cotangent.reshape(DEVICES, NODES_DEV, HID)
    tile_blocks = tile_values.reshape(DEVICES, TILES, TILE, TILE)
    hidden_rows, weight_part, own_grad, halo_grad = lax.map(lambda packed: local_pass(packed, weight), (own_rows, halo_sub, halo_dom, grad_out, tile_index, tile_count, tile_blocks))
    weight_grad = lax.optimization_barrier(jnp.sum(weight_part, axis=0)) / jnp.sqrt(jnp.float32(NODES))
    sub_grad = halo_grad[:, :N_SUB * SS].reshape(N_DOM, N_SUB, N_SUB, SS, F).transpose(0, 2, 1, 3, 4)
    dom_grad = halo_grad[:, N_SUB * SS:].reshape(N_DOM, N_SUB, N_DOM, SD, F).transpose(2, 1, 0, 3, 4)
    offsets = (jnp.arange(DEVICES, dtype=jnp.int32) * NODES_DEV).reshape(N_DOM, N_SUB, 1, 1)
    sub_target = (sub_lists + offsets).astype(jnp.int32)
    dom_target = (dom_lists + offsets).astype(jnp.int32)
    grad_total = own_grad.reshape(NODES, F)
    grad_total = grad_total.at[sub_target.reshape(-1)].add(sub_grad.reshape(-1, F))
    grad_total = grad_total.at[dom_target.reshape(-1)].add(dom_grad.reshape(-1, F))
    return (hidden_rows.reshape(NODES, HID), weight_grad, grad_total.astype(jnp.bfloat16))
```

```python
import functools

import jax
import jax.numpy as jnp
from jax import lax
from jax.experimental import pallas as pl
from jax.experimental.pallas import tpu as pltpu
from jax.sharding import PartitionSpec as P

BF = jnp.bfloat16
F32 = jnp.float32
I32 = jnp.int32
MESH = pl.DeviceIdType.MESH


def iota(shape, dim):
    return lax.broadcasted_iota(I32, shape, dim)


def dot(a, b):
    return jnp.dot(a, b, preferred_element_type=F32)


def dot_tn(a, b):
    return lax.dot_general(a, b, (((0,), (0,)), ((), ())), preferred_element_type=F32)


def dot_nt(a, b):
    return lax.dot_general(a, b, (((1,), (1,)), ((), ())), preferred_element_type=F32)


def slot_order(t, rb, nh):
    return jnp.where(t < nh, t + rb, jnp.where(t < nh + rb, t - nh, t))


def kernel(
    c,
    feats, stale, weight, cot, send_sub, send_dom, meta_s, tiles_hbm,
    hidden, wgrad, fgrad,
    st, xcols, tiles, cotv, chain, gbuf, aggv, gzv,
    ohg, ohs, sub_out, g_out, g_in, z_out, back, rsub, rz, rg_out, rg_in, rdom,
    wpart, py, pg_out, pg, pz_out, pz, ag, agy,
    sem_in, ss, rs,
):
    ns, ng, nz, tile, rb, nh, slots = c.ns, c.ng, c.nz, c.tile, c.rb, c.nh, c.slots
    rows, cb, ssub, sdom = c.rows, c.cb, c.ssub, c.sdom
    sub_total, dom_total = ns * ssub, ng * nz * sdom
    gpad = c.gpad
    d = lax.axis_index("dom")
    me_s = lax.axis_index("sub")
    me_z, me_g = d // ng, d % ng

    stale_cp = pltpu.make_async_copy(stale, st, sem_in.at[0])
    feats_cp = pltpu.make_async_copy(feats, xcols.at[pl.ds(0, rb)], sem_in.at[1])
    tiles_cp = pltpu.make_async_copy(tiles_hbm, tiles, sem_in.at[2])
    cot_cp = pltpu.make_async_copy(cot, cotv, sem_in.at[3])
    stale_cp.start()
    feats_cp.start()
    tiles_cp.start()
    cot_cp.start()

    def at_sub(k):
        peer = lax.rem(me_s + k, ns)
        return peer, {"dom": d, "sub": peer}

    def at_g(k):
        peer = lax.rem(me_g + k, ng)
        return peer, {"dom": me_z * ng + peer, "sub": me_s}

    def at_z(k):
        peer = lax.rem(me_z + k, nz)
        return peer, {"dom": peer * ng + me_g, "sub": me_s}

    barrier = pltpu.get_barrier_semaphore()
    for n, where in ((ng, at_g), (nz, at_z), (ns, at_sub)):

        def greet(k, carry, where=where):
            pl.semaphore_signal(barrier, inc=1, device_id=where(k)[1], device_id_type=MESH)
            return carry

        lax.fori_loop(1, n, greet, 0)

    def exchange(phase, n, where, src, dst):
        def copy(k):
            peer, device = where(k)
            return pltpu.make_async_remote_copy(
                src_ref=src(peer),
                dst_ref=dst,
                send_sem=ss.at[phase, k],
                recv_sem=rs.at[phase, k],
                device_id=device,
                device_id_type=MESH,
            )

        def each(act):
            def step(k, carry):
                act(copy(k))
                return carry

            lax.fori_loop(1, n, step, 0)

        return (
            lambda: each(lambda m: m.start()),
            lambda: each(lambda m: m.wait_recv()),
            lambda: each(lambda m: m.wait_send()),
        )

    sub_t = jnp.transpose(jnp.concatenate([send_sub[...], jnp.zeros((ns, 128 - ssub), I32)], axis=1))
    lane_n = iota((1, rows), 1)
    for j in range(ns):
        ohg[j * ssub : (j + 1) * ssub, :] = (sub_t[:ssub, j : j + 1] == lane_n).astype(F32).astype(BF)
    nd = ng * nz
    dom_t = send_dom[...]
    dom_i = jnp.transpose(jnp.concatenate([dom_t, jnp.zeros((sdom, 128 - nd), I32)], axis=1))[:nd]
    for k in range(sdom):
        lo = sub_total + k * nd
        ohg[lo : lo + nd, :] = (dom_i[:, k : k + 1] == lane_n).astype(F32).astype(BF)
    stale_cp.wait()
    picked = dot(ohg[sub_total : sub_total + dom_total, :], st[...]).astype(BF)
    out_r = iota((ng * gpad, dom_total), 0)
    in_r = iota((ng * gpad, dom_total), 1)
    og, ozk = out_r // gpad, out_r % gpad
    want = (ozk % sdom) * nd + (ozk // sdom) * ng + og
    perm = ((want == in_r) & (ozk < nz * sdom)).astype(F32).astype(BF)
    g_out[...] = dot(perm, picked).astype(BF).reshape(g_out.shape)
    pl.semaphore_wait(barrier, ns + ng + nz - 3)
    fg = exchange(0, ng, at_g, lambda p: g_out.at[p], g_in.at[me_g])
    fg[0]()
    g_in[pl.ds(me_g, 1)] = g_out[pl.ds(me_g, 1)]
    sub_out[...] = dot(ohg[0:sub_total, :], st[...]).astype(BF).reshape(sub_out.shape)
    per = tile // ssub
    sub_at = xcols.at[rb + me_s // per, pl.ds(pl.multiple_of(me_s % per * ssub, 16), ssub)]
    fs = exchange(1, ns, at_sub, lambda p: sub_out.at[p], sub_at)
    fs[0]()
    sub_at[...] = sub_out[me_s]
    spare = (sub_total + dom_total) % tile
    if spare:
        xcols[cb - 1, spare:, :] = jnp.zeros((tile - spare, xcols.shape[2]), BF)

    fg[1]()
    out_r = iota((dom_total, ng * gpad), 0)
    in_r = iota((dom_total, ng * gpad), 1)
    oz, ogk = out_r // (ng * sdom), out_r % (ng * sdom)
    want = (ogk // sdom) * gpad + oz * sdom + ogk % sdom
    turn_z = (want == in_r).astype(F32).astype(BF)
    z_out[...] = dot(turn_z, g_in[...].reshape(ng * gpad, -1)).astype(BF).reshape(z_out.shape)
    zrows = ng * sdom
    z_row = sub_total + me_z * zrows
    z_at = xcols.at[rb + z_row // tile, pl.ds(pl.multiple_of(z_row % tile, 16), zrows)]
    fz = exchange(2, nz, at_z, lambda p: z_out.at[p], z_at)
    fz[0]()
    z_at[...] = z_out[me_z]

    feats_cp.wait()
    tiles_cp.wait()
    for p in range(rb):
        chain[p] = dot(tiles[nh + p], xcols[p])
    cot_cp.wait()
    node = iota((rows, 1), 0)
    for j in range(ns):
        ohs[:, j * ssub : (j + 1) * ssub] = (send_sub[j : j + 1, :] == node).astype(F32).astype(BF)
    fs[1]()
    fz[1]()

    for s in (*range(nh), *range(nh + rb, slots)):
        p = s + rb if s < nh else s
        if s < nh:
            block = xcols[rb + s]
        else:
            block = xcols[meta_s[1, s]]
        chain[p] = dot(tiles[s], block) + chain[meta_s[2, s]]

    step = c.step
    w = weight[...]
    for b in range(rb // step):
        lo, hi = b * step * tile, (b + 1) * step * tile
        for r in range(b * step, (b + 1) * step):
            aggv[r * tile : (r + 1) * tile, :] = chain[meta_s[3, r]].astype(BF)
        agg = aggv[lo:hi, :]
        pre = dot(agg, w)
        sig = jax.nn.sigmoid(pre)
        hidden[lo:hi, :] = (pre * sig).astype(BF)
        gz = (cotv[lo:hi, :].astype(F32) * sig * (1.0 + pre * (1.0 - sig))).astype(BF)
        gzv[lo:hi, :] = gz
        gbuf[b * step : (b + 1) * step] = dot_nt(gz, w).astype(BF).reshape(step, tile, -1)
    wpart[...] = dot_tn(aggv[...], gzv[...]).reshape(wpart.shape)
    w1 = exchange(3, ns, at_sub, lambda p: wpart.at[p], py.at[me_s])
    w1[0]()
    py[pl.ds(me_s, 1)] = wpart[pl.ds(me_s, 1)]

    for s in range(slots):
        p = s + rb if s < nh else (s - nh if s < nh + rb else s)
        if nh <= s < nh + rb:
            block = gbuf[s - nh]
        else:
            block = gbuf[meta_s[0, s]]
        term = dot_tn(tiles[s], block)
        chain[p] = term if p < cb else term + chain[meta_s[4, s]]
    for h in range(nh):
        back[h * tile : (h + 1) * tile, :] = chain[meta_s[5, rb + h]].astype(BF)
    bz = exchange(4, nz, at_z, lambda p: back.at[pl.ds(pl.multiple_of(sub_total + p * zrows, 16), zrows)], rz.at[me_z])
    bz[0]()
    rz[pl.ds(me_z, 1)] = back[pl.ds(pl.multiple_of(sub_total + me_z * zrows, 16), zrows), :].reshape(1, zrows, -1)
    bs = exchange(5, ns, at_sub, lambda p: back.at[pl.ds(pl.multiple_of(p * ssub, 16), ssub)], rsub.at[pl.ds(pl.multiple_of(me_s * ssub, 16), ssub)])
    bs[0]()
    rsub[pl.ds(pl.multiple_of(me_s * ssub, 16), ssub), :] = back[pl.ds(pl.multiple_of(me_s * ssub, 16), ssub), :]

    w1[1]()
    part = py[0]
    for i in range(1, ns):
        part = part + py[i]
    rg = part.shape[0] // ng
    for i in range(ng):
        pg_out[i] = part[i * rg : (i + 1) * rg, :]
    w2 = exchange(6, ng, at_g, lambda p: pg_out.at[p], pg.at[me_g])
    w2[0]()
    pg[pl.ds(me_g, 1)] = pg_out[pl.ds(me_g, 1)]

    bz[1]()
    out_r = iota((ng * gpad, dom_total), 0)
    in_r = iota((ng * gpad, dom_total), 1)
    og, ozk = out_r // gpad, out_r % gpad
    want = (ozk // sdom) * zrows + og * sdom + ozk % sdom
    turn_g = ((want == in_r) & (ozk < nz * sdom)).astype(F32).astype(BF)
    rg_out[...] = dot(turn_g, rz[...].reshape(dom_total, -1)).astype(BF).reshape(rg_out.shape)
    bg = exchange(7, ng, at_g, lambda p: rg_out.at[p], rg_in.at[me_g])
    bg[0]()
    rg_in[pl.ds(me_g, 1)] = rg_out[pl.ds(me_g, 1)]

    w2[1]()
    part = pg[0]
    for i in range(1, ng):
        part = part + pg[i]
    pz_out[...] = part
    w3 = exchange(8, nz, at_z, lambda p: pz_out, pz.at[me_z])
    w3[0]()
    pz[pl.ds(me_z, 1)] = part[None]

    bs[1]()
    bg[1]()
    out_r = iota((dom_total, ng * gpad), 0)
    in_r = iota((dom_total, ng * gpad), 1)
    ok, ozg = out_r // nd, out_r % nd
    want = (ozg % ng) * gpad + (ozg // ng) * sdom + ok
    turn_k = (want == in_r).astype(F32).astype(BF)
    rdom[...] = dot(turn_k, rg_in[...].reshape(ng * gpad, -1)).astype(BF)

    w3[1]()
    part = pz[0]
    for i in range(1, nz):
        part = part + pz[i]
    part = part * c.scale
    pz_out2 = pg_out.at[0]
    w2[2]()
    pz_out2[...] = part
    w4 = exchange(9, ng, at_g, lambda p: pz_out2, ag.at[me_g])
    w4[0]()
    ag[pl.ds(me_g, 1)] = part[None]

    def total(b):
        lo, hi = b * step * tile, (b + 1) * step * tile
        acc = dot(ohs[lo:hi, 0:sub_total], rsub[...])
        node_b = lo + iota((hi - lo, 1), 0)
        for k in range(sdom):
            oh = (dom_t[k : k + 1, :] == node_b).astype(F32).astype(BF)
            acc = acc + dot(oh, rdom[k * nd : (k + 1) * nd, :])
        for r in range(step):
            x = chain[meta_s[5, b * step + r]] + acc[r * tile : (r + 1) * tile, :]
            fgrad[lo + r * tile : lo + (r + 1) * tile, :] = x.astype(BF)

    n_b = rb // step
    for b in range(n_b // 2):
        total(b)

    w4[1]()
    w1[2]()
    for i in range(ng):
        wpart[0, i * rg : (i + 1) * rg, :] = ag[i]
    w5 = exchange(10, ns, at_sub, lambda p: wpart.at[0], agy.at[me_s])
    w5[0]()
    agy[pl.ds(me_s, 1)] = wpart[0:1]
    for b in range(n_b // 2, n_b):
        total(b)
    w5[1]()
    wgrad[...] = agy[...].reshape(wgrad.shape)
    for x in (fg, fs, fz, bz, bs, bg, w3, w4, w5):
        x[2]()


def slot_chains(rb, nh, slots, tile_index, tile_count, out):
    out[...] = jnp.zeros_like(out)
    out[0:2, 0:slots] = tile_index[0]
    lanes = out.shape[1]
    count = tile_count[0]
    picks = out[...]
    u = iota((lanes, lanes), 0)
    t = iota((lanes, lanes), 1)
    ord_u = slot_order(u, rb, nh)
    ord_t = slot_order(t, rb, nh)
    for which in range(2):
        line = jnp.broadcast_to(picks[which : which + 1, :], (lanes, lanes))
        turned = line.T
        prev = jnp.where((turned == line) & (ord_u < ord_t) & (u < slots), ord_u, 0)
        last = jnp.where((turned == t) & (u < count), ord_u, 0)
        out[2 + 2 * which : 3 + 2 * which, :] = jnp.max(prev, axis=0, keepdims=True)
        out[3 + 2 * which : 4 + 2 * which, :] = jnp.max(last, axis=0, keepdims=True)


class Sizes:
    pass


def on_device(feats, stale, weight, cot, send_sub, send_dom, tile_index, tile_count, tiles):
    c = Sizes()
    c.rows, f = feats.shape
    c.slots, c.tile = tiles.shape[0], tiles.shape[1]
    c.rb = c.rows // c.tile
    c.ns, c.ssub = send_sub.shape
    nd, c.sdom = send_dom.shape
    c.ng = 16 // c.sdom
    c.nz = nd // c.ng
    halo = c.ns * c.ssub + nd * c.sdom
    c.nh = -(-halo // c.tile)
    c.cb = c.rb + c.nh
    c.gpad = -(-c.nz * c.sdom // 16) * 16
    c.step = max(1, c.rb // 4)
    c.scale = float(1.0 / (c.rows * nd * c.ns) ** 0.5)
    hid = weight.shape[1]
    sub_total, dom_total = c.ns * c.ssub, nd * c.sdom
    ry = f // c.ns
    rg = ry // c.ng
    vmem = pl.BlockSpec(memory_space=pltpu.VMEM)
    smem = pl.BlockSpec(memory_space=pltpu.SMEM)
    hbm = pl.BlockSpec(memory_space=pltpu.HBM)
    meta = pl.pallas_call(
        functools.partial(slot_chains, c.rb, c.nh, c.slots),
        out_shape=jax.ShapeDtypeStruct((8, 128), I32),
        in_specs=[vmem, smem],
        out_specs=vmem,
    )(tile_index, tile_count)
    scratch = [
        pltpu.VMEM((c.rows, f), BF),
        pltpu.VMEM((c.cb, c.tile, f), BF),
        pltpu.VMEM((c.slots, c.tile, c.tile), BF),
        pltpu.VMEM((c.rows, hid), BF),
        pltpu.VMEM((c.slots, c.tile, f), F32),
        pltpu.VMEM((c.rb, c.tile, f), BF),
        pltpu.VMEM((c.rows, f), BF),
        pltpu.VMEM((c.rows, hid), BF),
        pltpu.VMEM((sub_total + dom_total, c.rows), BF),
        pltpu.VMEM((c.rows, sub_total), BF),
        pltpu.VMEM((c.ns, c.ssub, f), BF),
        pltpu.VMEM((c.ng, c.gpad, f), BF),
        pltpu.VMEM((c.ng, c.gpad, f), BF),
        pltpu.VMEM((c.nz, c.ng * c.sdom, f), BF),
        pltpu.VMEM((c.nh * c.tile, f), BF),
        pltpu.VMEM((sub_total, f), BF),
        pltpu.VMEM((c.nz, c.ng * c.sdom, f), BF),
        pltpu.VMEM((c.ng, c.gpad, f), BF),
        pltpu.VMEM((c.ng, c.gpad, f), BF),
        pltpu.VMEM((dom_total, f), BF),
        pltpu.VMEM((c.ns, ry, hid), F32),
        pltpu.VMEM((c.ns, ry, hid), F32),
        pltpu.VMEM((c.ng, rg, hid), F32),
        pltpu.VMEM((c.ng, rg, hid), F32),
        pltpu.VMEM((rg, hid), F32),
        pltpu.VMEM((c.nz, rg, hid), F32),
        pltpu.VMEM((c.ng, rg, hid), F32),
        pltpu.VMEM((c.ns, ry, hid), F32),
        pltpu.SemaphoreType.DMA((4,)),
        pltpu.SemaphoreType.DMA((11, max(c.ns, c.ng, c.nz))),
        pltpu.SemaphoreType.DMA((11, max(c.ns, c.ng, c.nz))),
    ]
    return pl.pallas_call(
        functools.partial(kernel, c),
        out_shape=(
            jax.ShapeDtypeStruct((c.rows, hid), BF),
            jax.ShapeDtypeStruct((f, hid), F32),
            jax.ShapeDtypeStruct((c.rows, f), BF),
        ),
        in_specs=[hbm, hbm, vmem, hbm, vmem, vmem, smem, hbm],
        out_specs=(vmem, vmem, vmem),
        scratch_shapes=scratch,
        compiler_params=pltpu.CompilerParams(
            collective_id=0, has_side_effects=True, vmem_limit_bytes=48 * 1024 * 1024
        ),
    )(feats.reshape(c.rb, c.tile, f), stale, weight, cot, send_sub, send_dom.T, meta, tiles)


def solution(mesh):
    rows = P(("dom", "sub"), None)
    cube = P(("dom", "sub"), None, None)
    return jax.shard_map(
        on_device,
        mesh=mesh,
        in_specs=(rows, rows, P(), rows, rows, rows, cube, P(("dom", "sub")), cube),
        out_specs=(rows, P(), rows),
        check_vma=False,
    )
```

```python
import functools

import jax
import jax.numpy as jnp
from jax import lax
from jax.experimental import pallas as pl
from jax.experimental.pallas import tpu as pltpu
from jax.sharding import PartitionSpec as P

BF = jnp.bfloat16
F32 = jnp.float32
I32 = jnp.int32
MESH = pl.DeviceIdType.MESH


def iota(shape, dim):
    return lax.broadcasted_iota(I32, shape, dim)


def dot(a, b):
    return jnp.dot(a, b, preferred_element_type=F32)


def dot_tn(a, b):
    return lax.dot_general(a, b, (((0,), (0,)), ((), ())), preferred_element_type=F32)


def dot_nt(a, b):
    return lax.dot_general(a, b, (((1,), (1,)), ((), ())), preferred_element_type=F32)


def one_hot(hit):
    return hit.astype(F32).astype(BF)


def slot_order(t, rb, nh):
    return jnp.where(t < nh, t + rb, jnp.where(t < nh + rb, t - nh, t))


def wrap(i, n):
    return jnp.where(i >= n, i - n, i)


class Exchange:
    def __init__(self, group, src, dst, block, ss, rs):
        self.copies = [
            pltpu.make_async_remote_copy(
                src_ref=src(peer), dst_ref=dst, send_sem=ss, recv_sem=rs, device_id=device, device_id_type=MESH
            )
            for peer, device in group
        ]
        self.block, self.ss, self.rs = block, ss, rs

    def start(self):
        for copy in self.copies:
            copy.start()

    def arrived(self):
        pltpu.make_async_copy(self.block, self.block, self.rs).wait()

    def left(self):
        pltpu.make_async_copy(self.block, self.block, self.ss).wait()


def kernel(
    c,
    feats, stale, weight, cot, send_sub, send_dom, meta_s, tiles_hbm,
    hidden_hbm, wgrad_hbm, fgrad_hbm,
    st, xcols, tiles, cotv, chain, gbuf, aggv, gzv,
    ohg, ohs, ohd, sub_out, g_out, g_in, z_out, back, rsub, rz, rg_out, rg_in, rdom,
    wp_out, wp_in, wm_out, wm_in, wa_out, wa_in, hidden, fgrad, wgrad, acc,
    sem_in, ss, rs,
):
    ns, ng, nz, tile, rb, nh, slots = c.ns, c.ng, c.nz, c.tile, c.rb, c.nh, c.slots
    rows, cb, ssub, sdom = c.rows, c.cb, c.ssub, c.sdom
    sub_total, dom_total = ns * ssub, ng * nz * sdom
    nd = ng * nz
    gpad, nl = c.gpad, c.nl
    d = lax.axis_index("dom")
    me_s = lax.axis_index("sub")
    me_z, me_g = d // ng, d % ng
    me_h, me_l = me_g // nl, me_g % nl

    stale_cp = pltpu.make_async_copy(stale, st, sem_in.at[0])
    feats_cp = pltpu.make_async_copy(feats, xcols.at[pl.ds(0, rb)], sem_in.at[1])
    tiles_cp = pltpu.make_async_copy(tiles_hbm, tiles, sem_in.at[2])
    cot_cp = pltpu.make_async_copy(cot, cotv, sem_in.at[3])
    hidden_cp = pltpu.make_async_copy(hidden, hidden_hbm, sem_in.at[4])
    fgrad_cp = pltpu.make_async_copy(fgrad, fgrad_hbm, sem_in.at[5])
    wgrad_cp = pltpu.make_async_copy(wgrad, wgrad_hbm, sem_in.at[6])
    stale_cp.start()
    feats_cp.start()
    tiles_cp.start()
    cot_cp.start()

    def along(*steps):
        sizes = (ns, nl, ng // nl, nz)
        mine = (me_s, me_l, me_h, me_z)
        offsets = [()]
        for axis in range(4):
            offsets = [o + (k,) for o in offsets for k in range(sizes[axis] if axis in steps else 1)]
        group = []
        for offset in offsets[1:]:
            at = [wrap(m + o, n) if o else m for m, o, n in zip(mine, offset, sizes)]
            index = 0
            for axis in reversed(range(4)):
                if axis in steps:
                    index = index * sizes[axis] + at[axis]
            s, l, h, z = at
            group.append((index, {"dom": (z * (ng // nl) + h) * nl + l, "sub": s}))
        return group

    by_sub, by_g, by_z = along(0), along(1, 2), along(3)
    by_piece, by_rest = along(0, 1), along(2, 3)
    barrier = pltpu.get_barrier_semaphore()
    for _, device in (*by_g, *by_z, *by_sub):
        pl.semaphore_signal(barrier, inc=1, device_id=device, device_id_type=MESH)

    lane_n = iota((1, rows), 1)
    dom_t = send_dom[...]
    dom_i = jnp.transpose(jnp.concatenate([dom_t, jnp.zeros((sdom, 128 - nd), I32)], axis=1))[:nd]
    for k in range(sdom):
        ohg[sub_total + k * nd : sub_total + (k + 1) * nd, :] = one_hot(dom_i[:, k : k + 1] == lane_n)
    stale_cp.wait()
    picked = dot(ohg[sub_total:, :], st[...]).astype(BF)
    out_r = iota((ng * gpad, dom_total), 0)
    in_r = iota((ng * gpad, dom_total), 1)
    og, ozk = out_r // gpad, out_r % gpad
    want = (ozk % sdom) * nd + (ozk // sdom) * ng + og
    perm = one_hot((want == in_r) & (ozk < nz * sdom))
    g_out[...] = dot(perm, picked).astype(BF).reshape(g_out.shape)
    pl.semaphore_wait(barrier, ns + ng + nz - 3)
    fg = Exchange(by_g, lambda p: g_out.at[p], g_in.at[me_g], g_in.at[pl.ds(0, ng - 1)], ss.at[0], rs.at[0])
    fg.start()
    g_in[pl.ds(me_g, 1)] = g_out[pl.ds(me_g, 1)]

    sub_t = jnp.transpose(jnp.concatenate([send_sub[...], jnp.zeros((ns, 128 - ssub), I32)], axis=1))
    for j in range(ns):
        ohg[j * ssub : (j + 1) * ssub, :] = one_hot(sub_t[:ssub, j : j + 1] == lane_n)
    sub_out[...] = dot(ohg[0:sub_total, :], st[...]).astype(BF).reshape(sub_out.shape)
    per = tile // ssub
    sub_at = xcols.at[rb + me_s // per, pl.ds(pl.multiple_of(me_s % per * ssub, 16), ssub)]
    fs = Exchange(by_sub, lambda p: sub_out.at[p], sub_at, sub_out.at[pl.ds(0, ns - 1)], ss.at[1], rs.at[1])
    fs.start()
    sub_at[...] = sub_out[me_s]
    spare = (sub_total + dom_total) % tile
    if spare:
        xcols[cb - 1, spare:, :] = jnp.zeros((tile - spare, xcols.shape[2]), BF)

    out_r = iota((dom_total, ng * gpad), 0)
    in_r = iota((dom_total, ng * gpad), 1)
    oz, ogk = out_r // (ng * sdom), out_r % (ng * sdom)
    want = (ogk // sdom) * gpad + oz * sdom + ogk % sdom
    turn_z = one_hot(want == in_r)
    fg.arrived()
    z_out[...] = dot(turn_z, g_in[...].reshape(ng * gpad, -1)).astype(BF).reshape(z_out.shape)
    zrows = ng * sdom
    z_row = sub_total + me_z * zrows
    z_at = xcols.at[rb + z_row // tile, pl.ds(pl.multiple_of(z_row % tile, 16), zrows)]
    fz = Exchange(by_z, lambda p: z_out.at[p], z_at, z_out.at[pl.ds(0, nz - 1)], ss.at[2], rs.at[2])
    fz.start()
    z_at[...] = z_out[me_z]

    feats_cp.wait()
    tiles_cp.wait()
    for p in range(rb):
        chain[p] = dot(tiles[nh + p], xcols[p])
    cot_cp.wait()
    node = iota((rows, 1), 0)
    for j in range(sub_total // 128):
        pieces = [send_sub[i : i + 1, :] for i in range(j * 128 // ssub, (j + 1) * 128 // ssub)]
        ohs[:, j * 128 : (j + 1) * 128] = one_hot(jnp.concatenate(pieces, axis=1) == node)
    ohd[...] = one_hot(jnp.concatenate([dom_t[k : k + 1, :] for k in range(sdom)], axis=1) == node)
    fs.arrived()
    fz.arrived()

    for s in (*range(nh), *range(nh + rb, slots)):
        p = s + rb if s < nh else s
        block = xcols[rb + s] if s < nh else xcols[meta_s[1, s]]
        chain[p] = dot(tiles[s], block) + chain[meta_s[2, s]]

    step = c.step
    w = weight[...]
    part = None
    for b in range(rb // step):
        lo, hi = b * step * tile, (b + 1) * step * tile
        for r in range(b * step, (b + 1) * step):
            aggv[r * tile : (r + 1) * tile, :] = chain[meta_s[3, r]].astype(BF)
        agg = aggv[lo:hi, :]
        pre = dot(agg, w)
        sig = jax.nn.sigmoid(pre)
        hidden[lo:hi, :] = (pre * sig).astype(BF)
        gz = (cotv[lo:hi, :].astype(F32) * sig * (1.0 + pre * (1.0 - sig))).astype(BF)
        gzv[lo:hi, :] = gz
        gbuf[b * step : (b + 1) * step] = dot_nt(gz, w).astype(BF).reshape(step, tile, -1)
    part = dot_tn(aggv[...], gzv[...])
    pieces = wp_out.shape[0]
    rp = wp_out.shape[1]
    for i in range(pieces):
        wp_out[i] = part[i * rp : (i + 1) * rp, :]

    me_p = me_l * ns + me_s
    w1 = Exchange(by_piece, lambda p: wp_out.at[p], wp_in.at[me_p], wp_in.at[pl.ds(0, pieces - 1)], ss.at[3], rs.at[3])
    w1.start()
    hidden_cp.start()
    wp_in[pl.ds(me_p, 1)] = wp_out[pl.ds(me_p, 1)]

    for s in range(slots):
        p = s + rb if s < nh else (s - nh if s < nh + rb else s)
        block = gbuf[s - nh] if nh <= s < nh + rb else gbuf[meta_s[0, s]]
        term = dot_tn(tiles[s], block)
        chain[p] = term if p < cb else term + chain[meta_s[4, s]]
    for h in range(nh):
        back[h * tile : (h + 1) * tile, :] = chain[meta_s[5, rb + h]].astype(BF)

    def back_z(p):
        return back.at[pl.ds(pl.multiple_of(sub_total + p * zrows, 16), zrows)]

    def back_s(p):
        return back.at[pl.ds(pl.multiple_of(p * ssub, 16), ssub)]

    bz = Exchange(by_z, back_z, rz.at[me_z], rz.at[pl.ds(0, nz - 1)], ss.at[4], rs.at[4])
    bz.start()
    bs = Exchange(by_sub, back_s, rsub.at[me_s], rsub.at[pl.ds(0, ns - 1)], ss.at[5], rs.at[5])
    bs.start()
    rz[pl.ds(me_z, 1)] = back_z(me_z)[...].reshape(1, zrows, -1)
    rsub[pl.ds(me_s, 1)] = back_s(me_s)[...].reshape(1, ssub, -1)
    out_r = iota((ng * gpad, dom_total), 0)
    in_r = iota((ng * gpad, dom_total), 1)
    og, ozk = out_r // gpad, out_r % gpad
    want = (ozk // sdom) * zrows + og * sdom + ozk % sdom
    turn_g = one_hot((want == in_r) & (ozk < nz * sdom))

    w1.arrived()
    piece = wp_in[0]
    for i in range(1, pieces):
        piece = piece + wp_in[i]
    wm_out[...] = piece
    rest = wm_in.shape[0]
    me_r = me_z * (ng // nl) + me_h
    w2 = Exchange(by_rest, lambda p: wm_out, wm_in.at[me_r], wm_in.at[pl.ds(0, rest - 1)], ss.at[6], rs.at[6])
    w2.start()
    wm_in[pl.ds(me_r, 1)] = piece[None]

    bz.arrived()
    rg_out[...] = dot(turn_g, rz[...].reshape(dom_total, -1)).astype(BF).reshape(rg_out.shape)
    bg = Exchange(by_g, lambda p: rg_out.at[p], rg_in.at[me_g], rg_in.at[pl.ds(0, ng - 1)], ss.at[7], rs.at[7])
    bg.start()
    rg_in[pl.ds(me_g, 1)] = rg_out[pl.ds(me_g, 1)]

    bs.arrived()
    for b in range(rb // step):
        lo, hi = b * step * tile, (b + 1) * step * tile
        got = dot(ohs[lo:hi, :], rsub[...].reshape(sub_total, -1))
        for r in range(step):
            acc[lo + r * tile : lo + (r + 1) * tile, :] = chain[meta_s[5, b * step + r]] + got[r * tile : (r + 1) * tile, :]

    out_r = iota((dom_total, ng * gpad), 0)
    in_r = iota((dom_total, ng * gpad), 1)
    ok, ozg = out_r // nd, out_r % nd
    want = (ozg % ng) * gpad + (ozg // ng) * sdom + ok
    turn_k = one_hot(want == in_r)
    bg.arrived()
    rdom[...] = dot(turn_k, rg_in[...].reshape(ng * gpad, -1)).astype(BF)
    for b in range(rb // step):
        lo, hi = b * step * tile, (b + 1) * step * tile
        fgrad[lo:hi, :] = (acc[lo:hi, :] + dot(ohd[lo:hi, :], rdom[...])).astype(BF)
    fgrad_cp.start()

    w2.arrived()
    piece = wm_in[0]
    for i in range(1, rest):
        piece = piece + wm_in[i]
    piece = piece * c.scale
    wa_out[...] = piece
    w3 = Exchange(by_piece, lambda p: wa_out, wa_in.at[me_p], wa_in.at[pl.ds(0, pieces - 1)], ss.at[8], rs.at[8])
    w3.start()
    wa_in[pl.ds(me_p, 1)] = piece[None]
    for x in (fg, fs, fz, bz, bs, bg, w1, w2):
        x.left()
    hidden_cp.wait()
    fgrad_cp.wait()
    w3.arrived()
    for i in range(pieces):
        wgrad[i * rp : (i + 1) * rp, :] = wa_in[i]
    wgrad_cp.start()
    w3.left()
    wgrad_cp.wait()


def hand_over(*refs):
    for src, dst in zip(refs[:3], refs[3:]):
        dst[...] = src[...]


def slot_chains(rb, nh, slots, tile_index, tile_count, out):
    out[...] = jnp.zeros_like(out)
    out[0:2, 0:slots] = tile_index[0]
    lanes = out.shape[1]
    count = tile_count[0]
    picks = out[...]
    u = iota((lanes, lanes), 0)
    t = iota((lanes, lanes), 1)
    ord_u = slot_order(u, rb, nh)
    ord_t = slot_order(t, rb, nh)
    for which in range(2):
        line = jnp.broadcast_to(picks[which : which + 1, :], (lanes, lanes))
        turned = line.T
        prev = jnp.where((turned == line) & (ord_u < ord_t) & (u < slots), ord_u, 0)
        last = jnp.where((turned == t) & (u < count), ord_u, 0)
        out[2 + 2 * which : 3 + 2 * which, :] = jnp.max(prev, axis=0, keepdims=True)
        out[3 + 2 * which : 4 + 2 * which, :] = jnp.max(last, axis=0, keepdims=True)


class Sizes:
    pass


def on_device(feats, stale, weight, cot, send_sub, send_dom, tile_index, tile_count, tiles):
    c = Sizes()
    c.rows, f = feats.shape
    c.slots, c.tile = tiles.shape[0], tiles.shape[1]
    c.rb = c.rows // c.tile
    c.ns, c.ssub = send_sub.shape
    nd, c.sdom = send_dom.shape
    c.ng = 16 // c.sdom
    c.nz = nd // c.ng
    halo = c.ns * c.ssub + nd * c.sdom
    c.nh = -(-halo // c.tile)
    c.cb = c.rb + c.nh
    c.gpad = -(-c.nz * c.sdom // 16) * 16
    c.step = max(1, c.rb // 4)
    c.scale = float(1.0 / (c.rows * nd * c.ns) ** 0.5)
    hid = weight.shape[1]
    sub_total, dom_total = c.ns * c.ssub, nd * c.sdom
    c.nl = max(1, c.ng // 2)
    pieces, rest = c.ns * c.nl, c.ng // c.nl * c.nz
    rp = f // pieces
    vmem = pl.BlockSpec(memory_space=pltpu.VMEM)
    smem = pl.BlockSpec(memory_space=pltpu.SMEM)
    hbm = pl.BlockSpec(memory_space=pltpu.HBM)
    meta = pl.pallas_call(
        functools.partial(slot_chains, c.rb, c.nh, c.slots),
        out_shape=jax.ShapeDtypeStruct((8, 128), I32),
        in_specs=[vmem, smem],
        out_specs=vmem,
    )(tile_index, tile_count)
    scratch = [
        pltpu.VMEM((c.rows, f), BF),
        pltpu.VMEM((c.cb, c.tile, f), BF),
        pltpu.VMEM((c.slots, c.tile, c.tile), BF),
        pltpu.VMEM((c.rows, hid), BF),
        pltpu.VMEM((c.slots, c.tile, f), F32),
        pltpu.VMEM((c.rb, c.tile, f), BF),
        pltpu.VMEM((c.rows, f), BF),
        pltpu.VMEM((c.rows, hid), BF),
        pltpu.VMEM((sub_total + dom_total, c.rows), BF),
        pltpu.VMEM((c.rows, sub_total), BF),
        pltpu.VMEM((c.rows, dom_total), BF),
        pltpu.VMEM((c.ns, c.ssub, f), BF),
        pltpu.VMEM((c.ng, c.gpad, f), BF),
        pltpu.VMEM((c.ng, c.gpad, f), BF),
        pltpu.VMEM((c.nz, c.ng * c.sdom, f), BF),
        pltpu.VMEM((c.nh * c.tile, f), BF),
        pltpu.VMEM((c.ns, c.ssub, f), BF),
        pltpu.VMEM((c.nz, c.ng * c.sdom, f), BF),
        pltpu.VMEM((c.ng, c.gpad, f), BF),
        pltpu.VMEM((c.ng, c.gpad, f), BF),
        pltpu.VMEM((dom_total, f), BF),
        pltpu.VMEM((pieces, rp, hid), F32),
        pltpu.VMEM((pieces, rp, hid), F32),
        pltpu.VMEM((rp, hid), F32),
        pltpu.VMEM((rest, rp, hid), F32),
        pltpu.VMEM((rp, hid), F32),
        pltpu.VMEM((pieces, rp, hid), F32),
        pltpu.VMEM((c.rows, hid), BF),
        pltpu.VMEM((c.rows, f), BF),
        pltpu.VMEM((f, hid), F32),
        pltpu.VMEM((c.rows, f), F32),
        pltpu.SemaphoreType.DMA((7,)),
        pltpu.SemaphoreType.DMA((9,)),
        pltpu.SemaphoreType.DMA((9,)),
    ]
    outs = (
        jax.ShapeDtypeStruct((c.rows, hid), BF),
        jax.ShapeDtypeStruct((f, hid), F32),
        jax.ShapeDtypeStruct((c.rows, f), BF),
    )
    results = pl.pallas_call(
        functools.partial(kernel, c),
        out_shape=outs,
        in_specs=[hbm, hbm, vmem, hbm, vmem, vmem, smem, hbm],
        out_specs=(hbm, hbm, hbm),
        scratch_shapes=scratch,
        compiler_params=pltpu.CompilerParams(
            collective_id=0, has_side_effects=True, vmem_limit_bytes=63 * 1024 * 1024
        ),
    )(feats.reshape(c.rb, c.tile, f), stale, weight, cot, send_sub, send_dom.T, meta, tiles)
    steps = 4
    blocks = [pl.BlockSpec((o.shape[0] // steps, o.shape[1]), lambda i: (i, 0)) for o in outs]
    return pl.pallas_call(
        hand_over,
        out_shape=outs,
        grid=(steps,),
        in_specs=blocks,
        out_specs=blocks,
    )(*results)


def solution(mesh):
    rows = P(("dom", "sub"), None)
    cube = P(("dom", "sub"), None, None)
    return jax.shard_map(
        on_device,
        mesh=mesh,
        in_specs=(rows, rows, P(), rows, rows, rows, cube, P(("dom", "sub")), cube),
        out_specs=(rows, P(), rows),
        check_vma=False,
    )
```

```python
import functools

import jax
import jax.numpy as jnp
from jax import lax
from jax.experimental import pallas as pl
from jax.experimental.pallas import tpu as pltpu
from jax.sharding import PartitionSpec as P

BF = jnp.bfloat16
F32 = jnp.float32
I32 = jnp.int32
MESH = pl.DeviceIdType.MESH


def iota(shape, dim):
    return lax.broadcasted_iota(I32, shape, dim)


def dot(a, b):
    return jnp.dot(a, b, preferred_element_type=F32)


def dot_tn(a, b):
    return lax.dot_general(a, b, (((0,), (0,)), ((), ())), preferred_element_type=F32)


def dot_nt(a, b):
    return lax.dot_general(a, b, (((1,), (1,)), ((), ())), preferred_element_type=F32)


def one_hot(hit):
    return hit.astype(F32).astype(BF)


def slot_order(t, rb, nh):
    return jnp.where(t < nh, t + rb, jnp.where(t < nh + rb, t - nh, t))


def wrap(i, n):
    return jnp.where(i >= n, i - n, i)


def slot_chains(rb, nh, slots, tile_index, tile_count, out):
    out[...] = jnp.zeros_like(out)
    out[0:2, 0:slots] = tile_index[0]
    lanes = out.shape[1]
    count = tile_count[0]
    picks = out[...]
    u = iota((lanes, lanes), 0)
    t = iota((lanes, lanes), 1)
    ord_u = slot_order(u, rb, nh)
    ord_t = slot_order(t, rb, nh)
    for which in range(2):
        line = jnp.broadcast_to(picks[which : which + 1, :], (lanes, lanes))
        turned = line.T
        prev = jnp.where((turned == line) & (ord_u < ord_t) & (u < slots), ord_u, 0)
        last = jnp.where((turned == t) & (u < count), ord_u, 0)
        out[2 + 2 * which : 3 + 2 * which, :] = jnp.max(prev, axis=0, keepdims=True)
        out[3 + 2 * which : 4 + 2 * which, :] = jnp.max(last, axis=0, keepdims=True)


class Exchange:
    def __init__(self, group, src, dst, block, ss, rs):
        self.copies = [
            pltpu.make_async_remote_copy(
                src_ref=src(peer), dst_ref=dst, send_sem=ss, recv_sem=rs, device_id=device, device_id_type=MESH
            )
            for peer, device in group
        ]
        self.block, self.ss, self.rs = block, ss, rs

    def start(self):
        for copy in self.copies:
            copy.start()

    def arrived(self):
        pltpu.make_async_copy(self.block, self.block, self.rs).wait()

    def left(self):
        pltpu.make_async_copy(self.block, self.block, self.ss).wait()


def kernel(
    c,
    feats, stale, weight, cot, send_sub, send_dom, tile_index, tile_count, tiles_hbm,
    hidden, wgrad, fgrad,
    st, xcols, tiles, cotv, chain, gbuf, aggv, gzv,
    ohg, ohs, ohd, sub_out, g_out, g_in, z_out, back, rsub, rz, rg_out, rg_in, rdom,
    wp_out, wp_in, wm_out, wm_in, wa_out, wa_in, acc,
    meta_v, meta_s, sem_in, ss, rs,
):
    ns, ng, nz, tile, rb, nh, slots = c.ns, c.ng, c.nz, c.tile, c.rb, c.nh, c.slots
    rows, cb, ssub, sdom = c.rows, c.cb, c.ssub, c.sdom
    sub_total, dom_total = ns * ssub, ng * nz * sdom
    nd = ng * nz
    gpad, nl = c.gpad, c.nl
    d = lax.axis_index("dom")
    me_s = lax.axis_index("sub")
    me_z, me_g = d // ng, d % ng
    me_h, me_l = me_g // nl, me_g % nl

    stale_cp = pltpu.make_async_copy(stale, st, sem_in.at[0])
    feats_cp = pltpu.make_async_copy(feats, xcols.at[pl.ds(0, rb)], sem_in.at[1])
    tiles_cp = pltpu.make_async_copy(tiles_hbm, tiles, sem_in.at[2])
    cot_cp = pltpu.make_async_copy(cot, cotv, sem_in.at[3])
    stale_cp.start()
    feats_cp.start()
    tiles_cp.start()
    cot_cp.start()

    def along(*steps):
        sizes = (ns, nl, ng // nl, nz)
        mine = (me_s, me_l, me_h, me_z)
        offsets = [()]
        for axis in range(4):
            offsets = [o + (k,) for o in offsets for k in range(sizes[axis] if axis in steps else 1)]
        offsets = sorted(offsets[1:], key=lambda o: -c.hops(o))
        group = []
        for offset in offsets:
            at = [wrap(m + o, n) if o else m for m, o, n in zip(mine, offset, sizes)]
            index = 0
            for axis in reversed(range(4)):
                if axis in steps:
                    index = index * sizes[axis] + at[axis]
            s, l, h, z = at
            group.append((index, {"dom": (z * (ng // nl) + h) * nl + l, "sub": s}))
        return group

    by_sub, by_g, by_z = along(0), along(1, 2), along(3)
    by_piece, by_rest = along(0, 1), along(2, 3)
    barrier = pltpu.get_barrier_semaphore()
    for _, device in (*by_g, *by_z, *by_sub):
        pl.semaphore_signal(barrier, inc=1, device_id=device, device_id_type=MESH)

    lane_n = iota((1, rows), 1)
    dom_t = send_dom[...]
    dom_i = jnp.transpose(jnp.concatenate([dom_t, jnp.zeros((sdom, 128 - nd), I32)], axis=1))[:nd]
    for k in range(sdom):
        ohg[sub_total + k * nd : sub_total + (k + 1) * nd, :] = one_hot(dom_i[:, k : k + 1] == lane_n)
    stale_cp.wait()
    picked = dot(ohg[sub_total:, :], st[...]).astype(BF)
    out_r = iota((ng * gpad, dom_total), 0)
    in_r = iota((ng * gpad, dom_total), 1)
    og, ozk = out_r // gpad, out_r % gpad
    want = (ozk % sdom) * nd + (ozk // sdom) * ng + og
    perm = one_hot((want == in_r) & (ozk < nz * sdom))
    g_out[...] = dot(perm, picked).astype(BF).reshape(g_out.shape)
    pl.semaphore_wait(barrier, ns + ng + nz - 3)
    fg = Exchange(by_g, lambda p: g_out.at[p], g_in.at[me_g], g_in.at[pl.ds(0, ng - 1)], ss.at[0], rs.at[0])
    fg.start()
    g_in[pl.ds(me_g, 1)] = g_out[pl.ds(me_g, 1)]

    sub_t = jnp.transpose(jnp.concatenate([send_sub[...], jnp.zeros((ns, 128 - ssub), I32)], axis=1))
    for j in range(ns):
        ohg[j * ssub : (j + 1) * ssub, :] = one_hot(sub_t[:ssub, j : j + 1] == lane_n)
    sub_out[...] = dot(ohg[0:sub_total, :], st[...]).astype(BF).reshape(sub_out.shape)
    per = tile // ssub
    sub_at = xcols.at[rb + me_s // per, pl.ds(pl.multiple_of(me_s % per * ssub, 16), ssub)]
    fs = Exchange(by_sub, lambda p: sub_out.at[p], sub_at, sub_out.at[pl.ds(0, ns - 1)], ss.at[1], rs.at[1])
    fs.start()
    sub_at[...] = sub_out[me_s]
    spare = (sub_total + dom_total) % tile
    if spare:
        xcols[cb - 1, spare:, :] = jnp.zeros((tile - spare, xcols.shape[2]), BF)

    slot_chains(rb, nh, slots, tile_index, tile_count, meta_v)
    meta_cp = pltpu.make_async_copy(meta_v, meta_s, sem_in.at[4])
    meta_cp.start()

    out_r = iota((dom_total, ng * gpad), 0)
    in_r = iota((dom_total, ng * gpad), 1)
    oz, ogk = out_r // (ng * sdom), out_r % (ng * sdom)
    want = (ogk // sdom) * gpad + oz * sdom + ogk % sdom
    turn_z = one_hot(want == in_r)
    fg.arrived()
    z_out[...] = dot(turn_z, g_in[...].reshape(ng * gpad, -1)).astype(BF).reshape(z_out.shape)
    zrows = ng * sdom
    z_row = sub_total + me_z * zrows
    z_at = xcols.at[rb + z_row // tile, pl.ds(pl.multiple_of(z_row % tile, 16), zrows)]
    fz = Exchange(by_z, lambda p: z_out.at[p], z_at, z_out.at[pl.ds(0, nz - 1)], ss.at[2], rs.at[2])
    fz.start()
    z_at[...] = z_out[me_z]

    feats_cp.wait()
    tiles_cp.wait()
    for p in range(rb):
        chain[p] = dot(tiles[nh + p], xcols[p])
    cot_cp.wait()
    node = iota((rows, 1), 0)
    for j in range(sub_total // 128):
        pieces = [send_sub[i : i + 1, :] for i in range(j * 128 // ssub, (j + 1) * 128 // ssub)]
        ohs[:, j * 128 : (j + 1) * 128] = one_hot(jnp.concatenate(pieces, axis=1) == node)
    ohd[...] = one_hot(jnp.concatenate([dom_t[k : k + 1, :] for k in range(sdom)], axis=1) == node)
    meta_cp.wait()
    fs.arrived()

    for s in (*range(nh), *range(nh + rb, slots)):
        if s == sub_total // tile:
            fz.arrived()
        p = s + rb if s < nh else s
        block = xcols[rb + s] if s < nh else xcols[meta_s[1, s]]
        chain[p] = dot(tiles[s], block) + chain[meta_s[2, s]]

    step = c.step
    w = weight[...]
    part = None
    for b in range(rb // step):
        lo, hi = b * step * tile, (b + 1) * step * tile
        for r in range(b * step, (b + 1) * step):
            aggv[r * tile : (r + 1) * tile, :] = chain[meta_s[3, r]].astype(BF)
        agg = aggv[lo:hi, :]
        pre = dot(agg, w)
        sig = jax.nn.sigmoid(pre)
        hidden[lo:hi, :] = (pre * sig).astype(BF)
        gz = (cotv[lo:hi, :].astype(F32) * sig * (1.0 + pre * (1.0 - sig))).astype(BF)
        gzv[lo:hi, :] = gz
        gbuf[b * step : (b + 1) * step] = dot_nt(gz, w).astype(BF).reshape(step, tile, -1)
    part = dot_tn(aggv[...], gzv[...])
    pieces = wp_out.shape[0]
    rp = wp_out.shape[1]
    for i in range(pieces):
        wp_out[i] = part[i * rp : (i + 1) * rp, :]

    me_p = me_l * ns + me_s
    w1 = Exchange(by_piece, lambda p: wp_out.at[p], wp_in.at[me_p], wp_in.at[pl.ds(0, pieces - 1)], ss.at[3], rs.at[3])
    w1.start()
    wp_in[pl.ds(me_p, 1)] = wp_out[pl.ds(me_p, 1)]

    for s in range(slots):
        p = s + rb if s < nh else (s - nh if s < nh + rb else s)
        block = gbuf[s - nh] if nh <= s < nh + rb else gbuf[meta_s[0, s]]
        term = dot_tn(tiles[s], block)
        chain[p] = term if p < cb else term + chain[meta_s[4, s]]
    for h in range(nh):
        back[h * tile : (h + 1) * tile, :] = chain[meta_s[5, rb + h]].astype(BF)

    def back_z(p):
        return back.at[pl.ds(pl.multiple_of(sub_total + p * zrows, 16), zrows)]

    def back_s(p):
        return back.at[pl.ds(pl.multiple_of(p * ssub, 16), ssub)]

    bz = Exchange(by_z, back_z, rz.at[me_z], rz.at[pl.ds(0, nz - 1)], ss.at[4], rs.at[4])
    bz.start()
    bs = Exchange(by_sub, back_s, rsub.at[me_s], rsub.at[pl.ds(0, ns - 1)], ss.at[5], rs.at[5])
    bs.start()
    rz[pl.ds(me_z, 1)] = back_z(me_z)[...].reshape(1, zrows, -1)
    rsub[pl.ds(me_s, 1)] = back_s(me_s)[...].reshape(1, ssub, -1)
    out_r = iota((ng * gpad, dom_total), 0)
    in_r = iota((ng * gpad, dom_total), 1)
    og, ozk = out_r // gpad, out_r % gpad
    want = (ozk // sdom) * zrows + og * sdom + ozk % sdom
    turn_g = one_hot((want == in_r) & (ozk < nz * sdom))

    w1.arrived()
    piece = wp_in[0]
    for i in range(1, pieces):
        piece = piece + wp_in[i]
    wm_out[...] = piece
    rest = wm_in.shape[0]
    me_r = me_z * (ng // nl) + me_h
    w2 = Exchange(by_rest, lambda p: wm_out, wm_in.at[me_r], wm_in.at[pl.ds(0, rest - 1)], ss.at[6], rs.at[6])
    w2.start()
    wm_in[pl.ds(me_r, 1)] = piece[None]

    bz.arrived()
    rg_out[...] = dot(turn_g, rz[...].reshape(dom_total, -1)).astype(BF).reshape(rg_out.shape)
    bg = Exchange(by_g, lambda p: rg_out.at[p], rg_in.at[me_g], rg_in.at[pl.ds(0, ng - 1)], ss.at[7], rs.at[7])
    bg.start()
    rg_in[pl.ds(me_g, 1)] = rg_out[pl.ds(me_g, 1)]

    bs.arrived()
    for b in range(rb // step):
        lo, hi = b * step * tile, (b + 1) * step * tile
        got = dot(ohs[lo:hi, :], rsub[...].reshape(sub_total, -1))
        for r in range(step):
            acc[lo + r * tile : lo + (r + 1) * tile, :] = chain[meta_s[5, b * step + r]] + got[r * tile : (r + 1) * tile, :]

    out_r = iota((dom_total, ng * gpad), 0)
    in_r = iota((dom_total, ng * gpad), 1)
    ok, ozg = out_r // nd, out_r % nd
    want = (ozg % ng) * gpad + (ozg // ng) * sdom + ok
    turn_k = one_hot(want == in_r)
    bg.arrived()
    rdom[...] = dot(turn_k, rg_in[...].reshape(ng * gpad, -1)).astype(BF)
    for b in range(rb // step):
        lo, hi = b * step * tile, (b + 1) * step * tile
        fgrad[lo:hi, :] = (acc[lo:hi, :] + dot(ohd[lo:hi, :], rdom[...])).astype(BF)

    w2.arrived()
    piece = wm_in[0]
    for i in range(1, rest):
        piece = piece + wm_in[i]
    piece = piece * c.scale
    wa_out[...] = piece
    w3 = Exchange(by_piece, lambda p: wa_out, wa_in.at[me_p], wa_in.at[pl.ds(0, pieces - 1)], ss.at[8], rs.at[8])
    w3.start()
    wa_in[pl.ds(me_p, 1)] = piece[None]
    for x in (fg, fs, fz, bz, bs, bg, w1, w2):
        x.left()
    w3.arrived()
    for i in range(pieces):
        wgrad[i * rp : (i + 1) * rp, :] = wa_in[i]
    w3.left()


def hand_over(hidden, wgrad, fgrad, *rest):
    outs, sems = rest[:3], rest[3]
    copies = [
        pltpu.make_async_copy(src, dst, sems.at[i]) for i, (src, dst) in enumerate(zip((hidden, wgrad, fgrad), outs))
    ]
    for copy in copies:
        copy.start()
    for copy in copies:
        copy.wait()


class Sizes:
    def hops(self, offset):
        s, l, h, z = offset
        return min(s, self.ns - s) + l // 2 + 0.25 * (l % 2) + 2 * h + min(z, self.nz - z)


def on_device(feats, stale, weight, cot, send_sub, send_dom, tile_index, tile_count, tiles):
    c = Sizes()
    c.rows, f = feats.shape
    c.slots, c.tile = tiles.shape[0], tiles.shape[1]
    c.rb = c.rows // c.tile
    c.ns, c.ssub = send_sub.shape
    nd, c.sdom = send_dom.shape
    c.ng = 16 // c.sdom
    c.nz = nd // c.ng
    halo = c.ns * c.ssub + nd * c.sdom
    c.nh = -(-halo // c.tile)
    c.cb = c.rb + c.nh
    c.gpad = -(-c.nz * c.sdom // 16) * 16
    c.step = max(1, c.rb // 4)
    c.scale = float(1.0 / (c.rows * nd * c.ns) ** 0.5)
    hid = weight.shape[1]
    sub_total, dom_total = c.ns * c.ssub, nd * c.sdom
    c.nl = max(1, c.ng // 2)
    pieces, rest = c.ns * c.nl, c.ng // c.nl * c.nz
    rp = f // pieces
    vmem = pl.BlockSpec(memory_space=pltpu.VMEM)
    smem = pl.BlockSpec(memory_space=pltpu.SMEM)
    hbm = pl.BlockSpec(memory_space=pltpu.HBM)
    scratch = [
        pltpu.VMEM((c.rows, f), BF),
        pltpu.VMEM((c.cb, c.tile, f), BF),
        pltpu.VMEM((c.slots, c.tile, c.tile), BF),
        pltpu.VMEM((c.rows, hid), BF),
        pltpu.VMEM((c.slots, c.tile, f), F32),
        pltpu.VMEM((c.rb, c.tile, f), BF),
        pltpu.VMEM((c.rows, f), BF),
        pltpu.VMEM((c.rows, hid), BF),
        pltpu.VMEM((sub_total + dom_total, c.rows), BF),
        pltpu.VMEM((c.rows, sub_total), BF),
        pltpu.VMEM((c.rows, dom_total), BF),
        pltpu.VMEM((c.ns, c.ssub, f), BF),
        pltpu.VMEM((c.ng, c.gpad, f), BF),
        pltpu.VMEM((c.ng, c.gpad, f), BF),
        pltpu.VMEM((c.nz, c.ng * c.sdom, f), BF),
        pltpu.VMEM((c.nh * c.tile, f), BF),
        pltpu.VMEM((c.ns, c.ssub, f), BF),
        pltpu.VMEM((c.nz, c.ng * c.sdom, f), BF),
        pltpu.VMEM((c.ng, c.gpad, f), BF),
        pltpu.VMEM((c.ng, c.gpad, f), BF),
        pltpu.VMEM((dom_total, f), BF),
        pltpu.VMEM((pieces, rp, hid), F32),
        pltpu.VMEM((pieces, rp, hid), F32),
        pltpu.VMEM((rp, hid), F32),
        pltpu.VMEM((rest, rp, hid), F32),
        pltpu.VMEM((rp, hid), F32),
        pltpu.VMEM((pieces, rp, hid), F32),
        pltpu.VMEM((c.rows, f), F32),
        pltpu.VMEM((8, 128), I32),
        pltpu.SMEM((8, 128), I32),
        pltpu.SemaphoreType.DMA((5,)),
        pltpu.SemaphoreType.DMA((9,)),
        pltpu.SemaphoreType.DMA((9,)),
    ]
    outs = (
        jax.ShapeDtypeStruct((c.rows, hid), BF),
        jax.ShapeDtypeStruct((f, hid), F32),
        jax.ShapeDtypeStruct((c.rows, f), BF),
    )
    results = pl.pallas_call(
        functools.partial(kernel, c),
        out_shape=tuple(pltpu.VMEM(o.shape, o.dtype) for o in outs),
        in_specs=[hbm, hbm, vmem, hbm, vmem, vmem, vmem, smem, hbm],
        out_specs=(vmem, vmem, vmem),
        scratch_shapes=scratch,
        compiler_params=pltpu.CompilerParams(
            collective_id=0, has_side_effects=True, vmem_limit_bytes=62500 * 1024
        ),
    )(feats.reshape(c.rb, c.tile, f), stale, weight, cot, send_sub, send_dom.T, tile_index, tile_count, tiles)
    return pl.pallas_call(
        hand_over,
        out_shape=outs,
        in_specs=[vmem] * 3,
        out_specs=(hbm,) * 3,
        scratch_shapes=[pltpu.SemaphoreType.DMA((3,))],
        compiler_params=pltpu.CompilerParams(vmem_limit_bytes=2 * 1024 * 1024),
    )(*results)


def solution(mesh):
    rows = P(("dom", "sub"), None)
    cube = P(("dom", "sub"), None, None)
    return jax.shard_map(
        on_device,
        mesh=mesh,
        in_specs=(rows, rows, P(), rows, rows, rows, cube, P(("dom", "sub")), cube),
        out_specs=(rows, P(), rows),
        check_vma=False,
    )
```

```python
import functools

import jax
import jax.numpy as jnp
from jax import lax
from jax.experimental import pallas as pl
from jax.experimental.pallas import tpu as pltpu
from jax.sharding import PartitionSpec as P

BF = jnp.bfloat16
F32 = jnp.float32
I32 = jnp.int32
MESH = pl.DeviceIdType.MESH


def iota(shape, dim):
    return lax.broadcasted_iota(I32, shape, dim)


def dot(a, b):
    return jnp.dot(a, b, preferred_element_type=F32)


def dot_tn(a, b):
    return lax.dot_general(a, b, (((0,), (0,)), ((), ())), preferred_element_type=F32)


def dot_nt(a, b):
    return lax.dot_general(a, b, (((1,), (1,)), ((), ())), preferred_element_type=F32)


def one_hot(hit):
    return hit.astype(F32).astype(BF)


def slot_order(t, rb, nh):
    return jnp.where(t < nh, t + rb, jnp.where(t < nh + rb, t - nh, t))


def wrap(i, n):
    return jnp.where(i >= n, i - n, i)


def slot_chains(rb, nh, slots, tile_index, tile_count, out):
    out[...] = jnp.zeros_like(out)
    out[0:2, 0:slots] = tile_index[0]
    lanes = out.shape[1]
    count = tile_count[0]
    picks = out[...]
    u = iota((lanes, lanes), 0)
    t = iota((lanes, lanes), 1)
    ord_u = slot_order(u, rb, nh)
    ord_t = slot_order(t, rb, nh)
    for which in range(2):
        line = jnp.broadcast_to(picks[which : which + 1, :], (lanes, lanes))
        turned = line.T
        prev = jnp.where((turned == line) & (ord_u < ord_t) & (u < slots), ord_u, 0)
        last = jnp.where((turned == t) & (u < count), ord_u, 0)
        out[2 + 2 * which : 3 + 2 * which, :] = jnp.max(prev, axis=0, keepdims=True)
        out[3 + 2 * which : 4 + 2 * which, :] = jnp.max(last, axis=0, keepdims=True)


class Exchange:
    def __init__(self, group, src, dst, block, ss, rs):
        self.copies = [
            pltpu.make_async_remote_copy(
                src_ref=src(peer), dst_ref=dst, send_sem=ss, recv_sem=rs, device_id=device, device_id_type=MESH
            )
            for peer, device in group
        ]
        self.block, self.ss, self.rs = block, ss, rs

    def start(self):
        for copy in self.copies:
            copy.start()

    def arrived(self):
        pltpu.make_async_copy(self.block, self.block, self.rs).wait()

    def left(self):
        pltpu.make_async_copy(self.block, self.block, self.ss).wait()


def kernel(
    c,
    feats, stale, weight_hbm, cot, sub_hbm, dom_hbm, index_hbm, count_hbm, tiles_hbm,
    hidden, wgrad, fgrad,
    st, xcols, tiles, cotv, chain, gbuf, aggv, gzv,
    ohg, ohs, ohd, sub_out, g_out, g_in, z_out, back, rsub, rz, rg_out, rg_in, rdom,
    wp_out, wp_in, wm_out, wm_in, wa_out, wa_in, acc,
    meta_v, meta_s, weight, send_sub, send_dom, tile_index, tile_count, sem_in, ss, rs,
):
    ns, ng, nz, tile, rb, nh, slots = c.ns, c.ng, c.nz, c.tile, c.rb, c.nh, c.slots
    rows, cb, ssub, sdom = c.rows, c.cb, c.ssub, c.sdom
    sub_total, dom_total = ns * ssub, ng * nz * sdom
    nd = ng * nz
    gpad, nl = c.gpad, c.nl
    d = lax.axis_index("dom")
    me_s = lax.axis_index("sub")
    me_z, me_g = d // ng, d % ng
    me_h, me_l = me_g // nl, me_g % nl

    stale_cp = pltpu.make_async_copy(stale, st, sem_in.at[0])
    feats_cp = pltpu.make_async_copy(feats, xcols.at[pl.ds(0, rb)], sem_in.at[1])
    tiles_cp = pltpu.make_async_copy(tiles_hbm, tiles, sem_in.at[2])
    cot_cp = pltpu.make_async_copy(cot, cotv, sem_in.at[3])
    dom_cp = pltpu.make_async_copy(dom_hbm, send_dom, sem_in.at[5])
    sub_cp = pltpu.make_async_copy(sub_hbm, send_sub, sem_in.at[6])
    index_cp = pltpu.make_async_copy(index_hbm, tile_index, sem_in.at[7])
    count_cp = pltpu.make_async_copy(count_hbm, tile_count, sem_in.at[8])
    weight_cp = pltpu.make_async_copy(weight_hbm, weight, sem_in.at[9])
    dom_cp.start()
    stale_cp.start()
    sub_cp.start()
    index_cp.start()
    count_cp.start()
    weight_cp.start()
    feats_cp.start()
    tiles_cp.start()
    cot_cp.start()

    def along(*steps):
        sizes = (ns, nl, ng // nl, nz)
        mine = (me_s, me_l, me_h, me_z)
        offsets = [()]
        for axis in range(4):
            offsets = [o + (k,) for o in offsets for k in range(sizes[axis] if axis in steps else 1)]
        offsets = sorted(offsets[1:], key=lambda o: -c.hops(o))
        group = []
        for offset in offsets:
            at = [wrap(m + o, n) if o else m for m, o, n in zip(mine, offset, sizes)]
            index = 0
            for axis in reversed(range(4)):
                if axis in steps:
                    index = index * sizes[axis] + at[axis]
            s, l, h, z = at
            group.append((index, {"dom": (z * (ng // nl) + h) * nl + l, "sub": s}))
        return group

    by_sub, by_g, by_z = along(0), along(1, 2), along(3)
    by_piece, by_rest = along(0, 1), along(2, 3)
    barrier = pltpu.get_barrier_semaphore()
    for _, device in (*by_g, *by_z, *by_sub):
        pl.semaphore_signal(barrier, inc=1, device_id=device, device_id_type=MESH)

    lane_n = iota((1, rows), 1)
    dom_cp.wait()
    dom_t = send_dom[...]
    dom_i = jnp.transpose(jnp.concatenate([dom_t, jnp.zeros((sdom, 128 - nd), I32)], axis=1))[:nd]
    for k in range(sdom):
        ohg[sub_total + k * nd : sub_total + (k + 1) * nd, :] = one_hot(dom_i[:, k : k + 1] == lane_n)
    stale_cp.wait()
    picked = dot(ohg[sub_total:, :], st[...]).astype(BF)
    out_r = iota((ng * gpad, dom_total), 0)
    in_r = iota((ng * gpad, dom_total), 1)
    og, ozk = out_r // gpad, out_r % gpad
    want = (ozk % sdom) * nd + (ozk // sdom) * ng + og
    perm = one_hot((want == in_r) & (ozk < nz * sdom))
    g_out[...] = dot(perm, picked).astype(BF).reshape(g_out.shape)
    pl.semaphore_wait(barrier, ns + ng + nz - 3)
    fg = Exchange(by_g, lambda p: g_out.at[p], g_in.at[me_g], g_in.at[pl.ds(0, ng - 1)], ss.at[0], rs.at[0])
    fg.start()
    g_in[pl.ds(me_g, 1)] = g_out[pl.ds(me_g, 1)]

    sub_cp.wait()
    sub_t = jnp.transpose(jnp.concatenate([send_sub[...], jnp.zeros((ns, 128 - ssub), I32)], axis=1))
    for j in range(ns):
        ohg[j * ssub : (j + 1) * ssub, :] = one_hot(sub_t[:ssub, j : j + 1] == lane_n)
    sub_out[...] = dot(ohg[0:sub_total, :], st[...]).astype(BF).reshape(sub_out.shape)
    per = tile // ssub
    sub_at = xcols.at[rb + me_s // per, pl.ds(pl.multiple_of(me_s % per * ssub, 16), ssub)]
    fs = Exchange(by_sub, lambda p: sub_out.at[p], sub_at, sub_out.at[pl.ds(0, ns - 1)], ss.at[1], rs.at[1])
    fs.start()
    sub_at[...] = sub_out[me_s]
    spare = (sub_total + dom_total) % tile
    if spare:
        xcols[cb - 1, spare:, :] = jnp.zeros((tile - spare, xcols.shape[2]), BF)

    index_cp.wait()
    count_cp.wait()
    slot_chains(rb, nh, slots, tile_index, tile_count, meta_v)
    meta_cp = pltpu.make_async_copy(meta_v, meta_s, sem_in.at[4])
    meta_cp.start()

    out_r = iota((dom_total, ng * gpad), 0)
    in_r = iota((dom_total, ng * gpad), 1)
    oz, ogk = out_r // (ng * sdom), out_r % (ng * sdom)
    want = (ogk // sdom) * gpad + oz * sdom + ogk % sdom
    turn_z = one_hot(want == in_r)
    fg.arrived()
    z_out[...] = dot(turn_z, g_in[...].reshape(ng * gpad, -1)).astype(BF).reshape(z_out.shape)
    zrows = ng * sdom
    z_row = sub_total + me_z * zrows
    z_at = xcols.at[rb + z_row // tile, pl.ds(pl.multiple_of(z_row % tile, 16), zrows)]
    fz = Exchange(by_z, lambda p: z_out.at[p], z_at, z_out.at[pl.ds(0, nz - 1)], ss.at[2], rs.at[2])
    fz.start()
    z_at[...] = z_out[me_z]

    feats_cp.wait()
    tiles_cp.wait()
    for p in range(rb):
        chain[p] = dot(tiles[nh + p], xcols[p])
    cot_cp.wait()
    weight_cp.wait()
    node = iota((rows, 1), 0)
    for j in range(sub_total // 128):
        pieces = [send_sub[i : i + 1, :] for i in range(j * 128 // ssub, (j + 1) * 128 // ssub)]
        ohs[:, j * 128 : (j + 1) * 128] = one_hot(jnp.concatenate(pieces, axis=1) == node)
    ohd[...] = one_hot(jnp.concatenate([dom_t[k : k + 1, :] for k in range(sdom)], axis=1) == node)
    meta_cp.wait()
    fs.arrived()

    for s in (*range(nh), *range(nh + rb, slots)):
        if s == sub_total // tile:
            fz.arrived()
        p = s + rb if s < nh else s
        block = xcols[rb + s] if s < nh else xcols[meta_s[1, s]]
        chain[p] = dot(tiles[s], block) + chain[meta_s[2, s]]

    step = c.step
    w = weight[...]
    for b in range(rb // step):
        lo, hi = b * step * tile, (b + 1) * step * tile
        for r in range(b * step, (b + 1) * step):
            aggv[r * tile : (r + 1) * tile, :] = chain[meta_s[3, r]].astype(BF)
        agg = aggv[lo:hi, :]
        pre = dot(agg, w)
        sig = jax.nn.sigmoid(pre)
        hidden[lo:hi, :] = (pre * sig).astype(BF)
        gz = (cotv[lo:hi, :].astype(F32) * sig * (1.0 + pre * (1.0 - sig))).astype(BF)
        gzv[lo:hi, :] = gz
    part = dot_tn(aggv[...], gzv[...])
    pieces = wp_out.shape[0]
    rp = wp_out.shape[1]
    for i in range(pieces):
        wp_out[i] = part[i * rp : (i + 1) * rp, :]

    me_p = me_l * ns + me_s
    w1 = Exchange(by_piece, lambda p: wp_out.at[p], wp_in.at[me_p], wp_in.at[pl.ds(0, pieces - 1)], ss.at[3], rs.at[3])
    w1.start()
    wp_in[pl.ds(me_p, 1)] = wp_out[pl.ds(me_p, 1)]

    for b in range(rb // step):
        gz = gzv[b * step * tile : (b + 1) * step * tile, :]
        gbuf[b * step : (b + 1) * step] = dot_nt(gz, w).astype(BF).reshape(step, tile, -1)
    for s in range(slots):
        p = s + rb if s < nh else (s - nh if s < nh + rb else s)
        block = gbuf[s - nh] if nh <= s < nh + rb else gbuf[meta_s[0, s]]
        term = dot_tn(tiles[s], block)
        chain[p] = term if p < cb else term + chain[meta_s[4, s]]
    for h in range(nh):
        back[h * tile : (h + 1) * tile, :] = chain[meta_s[5, rb + h]].astype(BF)

    def back_z(p):
        return back.at[pl.ds(pl.multiple_of(sub_total + p * zrows, 16), zrows)]

    def back_s(p):
        return back.at[pl.ds(pl.multiple_of(p * ssub, 16), ssub)]

    bz = Exchange(by_z, back_z, rz.at[me_z], rz.at[pl.ds(0, nz - 1)], ss.at[4], rs.at[4])
    bz.start()
    bs = Exchange(by_sub, back_s, rsub.at[me_s], rsub.at[pl.ds(0, ns - 1)], ss.at[5], rs.at[5])
    bs.start()
    rz[pl.ds(me_z, 1)] = back_z(me_z)[...].reshape(1, zrows, -1)
    rsub[pl.ds(me_s, 1)] = back_s(me_s)[...].reshape(1, ssub, -1)
    out_r = iota((ng * gpad, dom_total), 0)
    in_r = iota((ng * gpad, dom_total), 1)
    og, ozk = out_r // gpad, out_r % gpad
    want = (ozk // sdom) * zrows + og * sdom + ozk % sdom
    turn_g = one_hot((want == in_r) & (ozk < nz * sdom))

    w1.arrived()
    piece = wp_in[0]
    for i in range(1, pieces):
        piece = piece + wp_in[i]
    wm_out[...] = piece
    rest = wm_in.shape[0]
    me_r = me_z * (ng // nl) + me_h
    w2 = Exchange(by_rest, lambda p: wm_out, wm_in.at[me_r], wm_in.at[pl.ds(0, rest - 1)], ss.at[6], rs.at[6])
    w2.start()
    wm_in[pl.ds(me_r, 1)] = piece[None]

    bz.arrived()
    rg_out[...] = dot(turn_g, rz[...].reshape(dom_total, -1)).astype(BF).reshape(rg_out.shape)
    bg = Exchange(by_g, lambda p: rg_out.at[p], rg_in.at[me_g], rg_in.at[pl.ds(0, ng - 1)], ss.at[7], rs.at[7])
    bg.start()
    rg_in[pl.ds(me_g, 1)] = rg_out[pl.ds(me_g, 1)]

    bs.arrived()
    for b in range(rb // step):
        lo, hi = b * step * tile, (b + 1) * step * tile
        got = dot(ohs[lo:hi, :], rsub[...].reshape(sub_total, -1))
        for r in range(step):
            acc[lo + r * tile : lo + (r + 1) * tile, :] = chain[meta_s[5, b * step + r]] + got[r * tile : (r + 1) * tile, :]

    w2.arrived()
    piece = wm_in[0]
    for i in range(1, rest):
        piece = piece + wm_in[i]
    piece = piece * c.scale
    wa_out[...] = piece
    w3 = Exchange(by_piece, lambda p: wa_out, wa_in.at[me_p], wa_in.at[pl.ds(0, pieces - 1)], ss.at[8], rs.at[8])
    w3.start()
    wa_in[pl.ds(me_p, 1)] = piece[None]

    out_r = iota((dom_total, ng * gpad), 0)
    in_r = iota((dom_total, ng * gpad), 1)
    ok, ozg = out_r // nd, out_r % nd
    want = (ozg % ng) * gpad + (ozg // ng) * sdom + ok
    turn_k = one_hot(want == in_r)
    bg.arrived()
    rdom[...] = dot(turn_k, rg_in[...].reshape(ng * gpad, -1)).astype(BF)
    for b in range(rb // step):
        lo, hi = b * step * tile, (b + 1) * step * tile
        fgrad[lo:hi, :] = (acc[lo:hi, :] + dot(ohd[lo:hi, :], rdom[...])).astype(BF)

    for x in (fg, fs, fz, bz, bs, bg, w1, w2):
        x.left()
    w3.arrived()
    for i in range(pieces):
        wgrad[i * rp : (i + 1) * rp, :] = wa_in[i]
    w3.left()


def hand_over(hidden, wgrad, fgrad, *rest):
    outs, sems = rest[:3], rest[3]
    copies = [
        pltpu.make_async_copy(src, dst, sems.at[i]) for i, (src, dst) in enumerate(zip((hidden, wgrad, fgrad), outs))
    ]
    for copy in copies:
        copy.start()
    for copy in copies:
        copy.wait()


class Sizes:
    def hops(self, offset):
        s, l, h, z = offset
        return min(s, self.ns - s) + l // 2 + 0.25 * (l % 2) + 2 * h + min(z, self.nz - z)


def on_device(feats, stale, weight, cot, send_sub, send_dom, tile_index, tile_count, tiles):
    c = Sizes()
    c.rows, f = feats.shape
    c.slots, c.tile = tiles.shape[0], tiles.shape[1]
    c.rb = c.rows // c.tile
    c.ns, c.ssub = send_sub.shape
    nd, c.sdom = send_dom.shape
    c.ng = 16 // c.sdom
    c.nz = nd // c.ng
    halo = c.ns * c.ssub + nd * c.sdom
    c.nh = -(-halo // c.tile)
    c.cb = c.rb + c.nh
    c.gpad = -(-c.nz * c.sdom // 16) * 16
    c.step = max(1, c.rb // 4)
    c.scale = float(1.0 / (c.rows * nd * c.ns) ** 0.5)
    hid = weight.shape[1]
    sub_total, dom_total = c.ns * c.ssub, nd * c.sdom
    c.nl = max(1, c.ng // 2)
    pieces, rest = c.ns * c.nl, c.ng // c.nl * c.nz
    rp = f // pieces
    vmem = pl.BlockSpec(memory_space=pltpu.VMEM)
    hbm = pl.BlockSpec(memory_space=pltpu.HBM)
    scratch = [
        pltpu.VMEM((c.rows, f), BF),
        pltpu.VMEM((c.cb, c.tile, f), BF),
        pltpu.VMEM((c.slots, c.tile, c.tile), BF),
        pltpu.VMEM((c.rows, hid), BF),
        pltpu.VMEM((c.slots, c.tile, f), F32),
        pltpu.VMEM((c.rb, c.tile, f), BF),
        pltpu.VMEM((c.rows, f), BF),
        pltpu.VMEM((c.rows, hid), BF),
        pltpu.VMEM((sub_total + dom_total, c.rows), BF),
        pltpu.VMEM((c.rows, sub_total), BF),
        pltpu.VMEM((c.rows, dom_total), BF),
        pltpu.VMEM((c.ns, c.ssub, f), BF),
        pltpu.VMEM((c.ng, c.gpad, f), BF),
        pltpu.VMEM((c.ng, c.gpad, f), BF),
        pltpu.VMEM((c.nz, c.ng * c.sdom, f), BF),
        pltpu.VMEM((c.nh * c.tile, f), BF),
        pltpu.VMEM((c.ns, c.ssub, f), BF),
        pltpu.VMEM((c.nz, c.ng * c.sdom, f), BF),
        pltpu.VMEM((c.ng, c.gpad, f), BF),
        pltpu.VMEM((c.ng, c.gpad, f), BF),
        pltpu.VMEM((dom_total, f), BF),
        pltpu.VMEM((pieces, rp, hid), F32),
        pltpu.VMEM((pieces, rp, hid), F32),
        pltpu.VMEM((rp, hid), F32),
        pltpu.VMEM((rest, rp, hid), F32),
        pltpu.VMEM((rp, hid), F32),
        pltpu.VMEM((pieces, rp, hid), F32),
        pltpu.VMEM((c.rows, f), F32),
        pltpu.VMEM((8, 128), I32),
        pltpu.SMEM((8, 128), I32),
        pltpu.VMEM((f, hid), BF),
        pltpu.VMEM((c.ns, c.ssub), I32),
        pltpu.VMEM((c.sdom, nd), I32),
        pltpu.VMEM((1, 2, c.slots), I32),
        pltpu.SMEM((1,), I32),
        pltpu.SemaphoreType.DMA((10,)),
        pltpu.SemaphoreType.DMA((9,)),
        pltpu.SemaphoreType.DMA((9,)),
    ]
    outs = (
        jax.ShapeDtypeStruct((c.rows, hid), BF),
        jax.ShapeDtypeStruct((f, hid), F32),
        jax.ShapeDtypeStruct((c.rows, f), BF),
    )
    results = pl.pallas_call(
        functools.partial(kernel, c),
        out_shape=tuple(pltpu.VMEM(o.shape, o.dtype) for o in outs),
        in_specs=[hbm] * 9,
        out_specs=(vmem, vmem, vmem),
        scratch_shapes=scratch,
        compiler_params=pltpu.CompilerParams(
            collective_id=0, has_side_effects=True, vmem_limit_bytes=62500 * 1024
        ),
    )(feats.reshape(c.rb, c.tile, f), stale, weight, cot, send_sub, send_dom.T, tile_index, tile_count, tiles)
    return pl.pallas_call(
        hand_over,
        out_shape=outs,
        in_specs=[vmem] * 3,
        out_specs=(hbm,) * 3,
        scratch_shapes=[pltpu.SemaphoreType.DMA((3,))],
        compiler_params=pltpu.CompilerParams(vmem_limit_bytes=2 * 1024 * 1024),
    )(*results)


def solution(mesh):
    rows = P(("dom", "sub"), None)
    cube = P(("dom", "sub"), None, None)
    return jax.shard_map(
        on_device,
        mesh=mesh,
        in_specs=(rows, rows, P(), rows, rows, rows, cube, P(("dom", "sub")), cube),
        out_specs=(rows, P(), rows),
        check_vma=False,
    )
```

```python
import functools

import jax
import jax.numpy as jnp
from jax import lax
from jax.experimental import pallas as pl
from jax.experimental.pallas import tpu as pltpu
from jax.sharding import PartitionSpec as P

BF = jnp.bfloat16
F32 = jnp.float32
I32 = jnp.int32
MESH = pl.DeviceIdType.MESH


def iota(shape, dim):
    return lax.broadcasted_iota(I32, shape, dim)


def dot(a, b):
    return jnp.dot(a, b, preferred_element_type=F32)


def dot_tn(a, b):
    return lax.dot_general(a, b, (((0,), (0,)), ((), ())), preferred_element_type=F32)


def dot_nt(a, b):
    return lax.dot_general(a, b, (((1,), (1,)), ((), ())), preferred_element_type=F32)


def one_hot(hit):
    return hit.astype(F32).astype(BF)


def slot_order(t, rb, nh):
    return jnp.where(t < nh, t + rb, jnp.where(t < nh + rb, t - nh, t))


def wrap(i, n):
    return jnp.where(i >= n, i - n, i)


def slot_chains(rb, nh, slots, tile_index, tile_count, out):
    out[...] = jnp.zeros_like(out)
    out[0:2, 0:slots] = tile_index[0]
    lanes = out.shape[1]
    count = tile_count[0]
    picks = out[...]
    u = iota((lanes, lanes), 0)
    t = iota((lanes, lanes), 1)
    ord_u = slot_order(u, rb, nh)
    ord_t = slot_order(t, rb, nh)
    for which in range(2):
        line = jnp.broadcast_to(picks[which : which + 1, :], (lanes, lanes))
        turned = line.T
        prev = jnp.where((turned == line) & (ord_u < ord_t) & (u < slots), ord_u, 0)
        last = jnp.where((turned == t) & (u < count), ord_u, 0)
        out[2 + 2 * which : 3 + 2 * which, :] = jnp.max(prev, axis=0, keepdims=True)
        out[3 + 2 * which : 4 + 2 * which, :] = jnp.max(last, axis=0, keepdims=True)


def total(terms):
    while len(terms) > 1:
        terms = [a + b for a, b in zip(terms[::2], terms[1::2])] + terms[len(terms) // 2 * 2 :]
    return terms[0]


class Exchange:
    def __init__(self, group, src, dst, block, ss, rs):
        self.copies = [
            pltpu.make_async_remote_copy(
                src_ref=src(peer), dst_ref=dst, send_sem=ss, recv_sem=rs, device_id=device, device_id_type=MESH
            )
            for peer, device in group
        ]
        self.block, self.ss, self.rs = block, ss, rs

    def start(self):
        for copy in self.copies:
            copy.start()

    def arrived(self):
        pltpu.make_async_copy(self.block, self.block, self.rs).wait()

    def left(self):
        pltpu.make_async_copy(self.block, self.block, self.ss).wait()


def kernel(
    c,
    feats, stale, weight_hbm, cot, sub_hbm, dom_hbm, index_hbm, count_hbm, tiles_hbm,
    hidden, wgrad, fgrad,
    st, xcols, tiles, cotv, chain, gbuf, aggv, gzv,
    ohg, ohs, ohd, sub_out, g_out, g_in, z_out, back, rsub, rz, rg_out, rg_in, rdom,
    wp_out, wp_in, wm_out, wm_in, wa_out, wa_in, acc,
    meta_v, meta_s, weight, send_sub, send_dom, tile_index, tile_count, sem_in, ss, rs,
):
    ns, ng, nz, tile, rb, nh, slots = c.ns, c.ng, c.nz, c.tile, c.rb, c.nh, c.slots
    rows, cb, ssub, sdom = c.rows, c.cb, c.ssub, c.sdom
    sub_total, dom_total = ns * ssub, ng * nz * sdom
    nd = ng * nz
    gpad, nl = c.gpad, c.nl
    d = lax.axis_index("dom")
    me_s = lax.axis_index("sub")
    me_z, me_g = d // ng, d % ng
    me_h, me_l = me_g // nl, me_g % nl

    stale_cp = pltpu.make_async_copy(stale, st, sem_in.at[0])
    feats_cp = pltpu.make_async_copy(feats, xcols.at[pl.ds(0, rb)], sem_in.at[1])
    tiles_cp = pltpu.make_async_copy(tiles_hbm, tiles, sem_in.at[2])
    cot_cp = pltpu.make_async_copy(cot, cotv, sem_in.at[3])
    dom_cp = pltpu.make_async_copy(dom_hbm, send_dom, sem_in.at[5])
    sub_cp = pltpu.make_async_copy(sub_hbm, send_sub, sem_in.at[6])
    index_cp = pltpu.make_async_copy(index_hbm, tile_index, sem_in.at[7])
    count_cp = pltpu.make_async_copy(count_hbm, tile_count, sem_in.at[8])
    weight_cp = pltpu.make_async_copy(weight_hbm, weight, sem_in.at[9])
    dom_cp.start()
    stale_cp.start()
    sub_cp.start()
    index_cp.start()
    count_cp.start()
    weight_cp.start()
    feats_cp.start()
    tiles_cp.start()
    cot_cp.start()

    def along(*steps):
        sizes = (ns, nl, ng // nl, nz)
        mine = (me_s, me_l, me_h, me_z)
        offsets = [()]
        for axis in range(4):
            offsets = [o + (k,) for o in offsets for k in range(sizes[axis] if axis in steps else 1)]
        offsets = sorted(offsets[1:], key=lambda o: -c.hops(o))
        group = []
        for offset in offsets:
            at = [wrap(m + o, n) if o else m for m, o, n in zip(mine, offset, sizes)]
            index = 0
            for axis in reversed(range(4)):
                if axis in steps:
                    index = index * sizes[axis] + at[axis]
            s, l, h, z = at
            group.append((index, {"dom": (z * (ng // nl) + h) * nl + l, "sub": s}))
        return group

    by_sub, by_g, by_z = along(0), along(1, 2), along(3)
    by_piece, by_rest = along(0, 1), along(2, 3)
    barrier = pltpu.get_barrier_semaphore()
    for _, device in (*by_g, *by_z, *by_sub):
        pl.semaphore_signal(barrier, inc=1, device_id=device, device_id_type=MESH)

    lane_n = iota((1, rows), 1)
    dom_cp.wait()
    dom_t = send_dom[...]
    dom_line = jnp.concatenate([dom_t[k : k + 1, :] for k in range(sdom)], axis=1)
    out_r = iota((ng * gpad, dom_total), 0)
    in_r = iota((ng * gpad, dom_total), 1)
    og, ozk = out_r // gpad, out_r % gpad
    want = (ozk % sdom) * nd + (ozk // sdom) * ng + og
    hit = (want == in_r) & (ozk < nz * sdom)
    dom_at = jnp.sum(jnp.where(hit, dom_line.astype(F32), 0.0), axis=1, keepdims=True)
    ohg[sub_total:, :] = one_hot(dom_at == lane_n.astype(F32))
    stale_cp.wait()
    g_out[...] = dot(ohg[sub_total:, :], st[...]).astype(BF).reshape(g_out.shape)
    pl.semaphore_wait(barrier, ns + ng + nz - 3)
    fg = Exchange(by_g, lambda p: g_out.at[p], g_in.at[me_g], g_in.at[pl.ds(0, ng - 1)], ss.at[0], rs.at[0])
    fg.start()
    g_in[pl.ds(me_g, 1)] = g_out[pl.ds(me_g, 1)]

    sub_cp.wait()
    sub_t = jnp.transpose(jnp.concatenate([send_sub[...], jnp.zeros((ns, 128 - ssub), I32)], axis=1))
    for j in range(ns):
        ohg[j * ssub : (j + 1) * ssub, :] = one_hot(sub_t[:ssub, j : j + 1] == lane_n)
    sub_out[...] = dot(ohg[0:sub_total, :], st[...]).astype(BF).reshape(sub_out.shape)
    per = tile // ssub
    sub_at = xcols.at[rb + me_s // per, pl.ds(pl.multiple_of(me_s % per * ssub, 16), ssub)]
    fs = Exchange(by_sub, lambda p: sub_out.at[p], sub_at, sub_out.at[pl.ds(0, ns - 1)], ss.at[1], rs.at[1])
    fs.start()
    sub_at[...] = sub_out[me_s]
    spare = (sub_total + dom_total) % tile
    if spare:
        xcols[cb - 1, spare:, :] = jnp.zeros((tile - spare, xcols.shape[2]), BF)

    index_cp.wait()
    count_cp.wait()
    slot_chains(rb, nh, slots, tile_index, tile_count, meta_v)
    meta_cp = pltpu.make_async_copy(meta_v, meta_s, sem_in.at[4])
    meta_cp.start()

    out_r = iota((dom_total, ng * gpad), 0)
    in_r = iota((dom_total, ng * gpad), 1)
    oz, ogk = out_r // (ng * sdom), out_r % (ng * sdom)
    want = (ogk // sdom) * gpad + oz * sdom + ogk % sdom
    turn_z = one_hot(want == in_r)
    fg.arrived()
    z_out[...] = dot(turn_z, g_in[...].reshape(ng * gpad, -1)).astype(BF).reshape(z_out.shape)
    zrows = ng * sdom
    z_row = sub_total + me_z * zrows
    z_at = xcols.at[rb + z_row // tile, pl.ds(pl.multiple_of(z_row % tile, 16), zrows)]
    fz = Exchange(by_z, lambda p: z_out.at[p], z_at, z_out.at[pl.ds(0, nz - 1)], ss.at[2], rs.at[2])
    fz.start()
    z_at[...] = z_out[me_z]

    feats_cp.wait()
    tiles_cp.wait()
    for p in range(rb):
        chain[p] = dot(tiles[nh + p], xcols[p])
    cot_cp.wait()
    weight_cp.wait()
    node = iota((rows, 1), 0)
    for j in range(sub_total // 128):
        pieces = [send_sub[i : i + 1, :] for i in range(j * 128 // ssub, (j + 1) * 128 // ssub)]
        ohs[:, j * 128 : (j + 1) * 128] = one_hot(jnp.concatenate(pieces, axis=1) == node)
    ohd[...] = one_hot(dom_line == node)
    meta_cp.wait()
    fs.arrived()

    for s in (*range(nh), *range(nh + rb, slots)):
        if s == sub_total // tile:
            fz.arrived()
        p = s + rb if s < nh else s
        block = xcols[rb + s] if s < nh else xcols[meta_s[1, s]]
        chain[p] = dot(tiles[s], block) + chain[meta_s[2, s]]

    step = c.step
    w = weight[...]
    for b in range(rb // step):
        lo, hi = b * step * tile, (b + 1) * step * tile
        for r in range(b * step, (b + 1) * step):
            aggv[r * tile : (r + 1) * tile, :] = chain[meta_s[3, r]].astype(BF)
        agg = aggv[lo:hi, :]
        pre = dot(agg, w)
        sig = jax.nn.sigmoid(pre)
        gz = (cotv[lo:hi, :].astype(F32) * sig * (1.0 + pre * (1.0 - sig))).astype(BF)
        gzv[lo:hi, :] = gz
    part = dot_tn(aggv[...], gzv[...])
    pieces = wp_out.shape[0]
    rp = wp_out.shape[1]
    for i in range(pieces):
        wp_out[i] = part[i * rp : (i + 1) * rp, :]

    me_p = me_l * ns + me_s
    w1 = Exchange(by_piece, lambda p: wp_out.at[p], wp_in.at[me_p], wp_in.at[pl.ds(0, pieces - 1)], ss.at[3], rs.at[3])
    w1.start()
    wp_in[pl.ds(me_p, 1)] = wp_out[pl.ds(me_p, 1)]

    for b in range(rb // step):
        gz = gzv[b * step * tile : (b + 1) * step * tile, :]
        gbuf[b * step : (b + 1) * step] = dot_nt(gz, w).astype(BF).reshape(step, tile, -1)
    for s in range(slots):
        p = s + rb if s < nh else (s - nh if s < nh + rb else s)
        block = gbuf[s - nh] if nh <= s < nh + rb else gbuf[meta_s[0, s]]
        term = dot_tn(tiles[s], block)
        chain[p] = term if p < cb else term + chain[meta_s[4, s]]
    for h in range(nh):
        back[h * tile : (h + 1) * tile, :] = chain[meta_s[5, rb + h]].astype(BF)

    def back_z(p):
        return back.at[pl.ds(pl.multiple_of(sub_total + p * zrows, 16), zrows)]

    def back_s(p):
        return back.at[pl.ds(pl.multiple_of(p * ssub, 16), ssub)]

    bz = Exchange(by_z, back_z, rz.at[me_z], rz.at[pl.ds(0, nz - 1)], ss.at[4], rs.at[4])
    bz.start()
    bs = Exchange(by_sub, back_s, rsub.at[me_s], rsub.at[pl.ds(0, ns - 1)], ss.at[5], rs.at[5])
    bs.start()
    rz[pl.ds(me_z, 1)] = back_z(me_z)[...].reshape(1, zrows, -1)
    rsub[pl.ds(me_s, 1)] = back_s(me_s)[...].reshape(1, ssub, -1)
    out_r = iota((ng * gpad, dom_total), 0)
    in_r = iota((ng * gpad, dom_total), 1)
    og, ozk = out_r // gpad, out_r % gpad
    want = (ozk // sdom) * zrows + og * sdom + ozk % sdom
    turn_g = one_hot((want == in_r) & (ozk < nz * sdom))

    w1.arrived()
    piece = total([wp_in[i] for i in range(pieces)])
    wm_out[...] = piece
    rest = wm_in.shape[0]
    me_r = me_z * (ng // nl) + me_h
    w2 = Exchange(by_rest, lambda p: wm_out, wm_in.at[me_r], wm_in.at[pl.ds(0, rest - 1)], ss.at[6], rs.at[6])
    w2.start()
    wm_in[pl.ds(me_r, 1)] = piece[None]

    bz.arrived()
    rg_out[...] = dot(turn_g, rz[...].reshape(dom_total, -1)).astype(BF).reshape(rg_out.shape)
    bg = Exchange(by_g, lambda p: rg_out.at[p], rg_in.at[me_g], rg_in.at[pl.ds(0, ng - 1)], ss.at[7], rs.at[7])
    bg.start()
    rg_in[pl.ds(me_g, 1)] = rg_out[pl.ds(me_g, 1)]

    for b in range(rb // step):
        lo, hi = b * step * tile, (b + 1) * step * tile
        pre = dot(aggv[lo:hi, :], w)
        hidden[lo:hi, :] = (pre * jax.nn.sigmoid(pre)).astype(BF)

    bs.arrived()
    for b in range(rb // step):
        lo, hi = b * step * tile, (b + 1) * step * tile
        got = dot(ohs[lo:hi, :], rsub[...].reshape(sub_total, -1))
        for r in range(step):
            acc[lo + r * tile : lo + (r + 1) * tile, :] = chain[meta_s[5, b * step + r]] + got[r * tile : (r + 1) * tile, :]

    w2.arrived()
    piece = total([wm_in[i] for i in range(rest)]) * c.scale
    wa_out[...] = piece
    w3 = Exchange(by_piece, lambda p: wa_out, wa_in.at[me_p], wa_in.at[pl.ds(0, pieces - 1)], ss.at[8], rs.at[8])
    w3.start()
    wa_in[pl.ds(me_p, 1)] = piece[None]

    out_r = iota((dom_total, ng * gpad), 0)
    in_r = iota((dom_total, ng * gpad), 1)
    ok, ozg = out_r // nd, out_r % nd
    want = (ozg % ng) * gpad + (ozg // ng) * sdom + ok
    turn_k = one_hot(want == in_r)
    bg.arrived()
    rdom[...] = dot(turn_k, rg_in[...].reshape(ng * gpad, -1)).astype(BF)
    for b in range(rb // step):
        lo, hi = b * step * tile, (b + 1) * step * tile
        fgrad[lo:hi, :] = (acc[lo:hi, :] + dot(ohd[lo:hi, :], rdom[...])).astype(BF)

    for x in (fg, fs, fz, bz, bs, bg, w1, w2):
        x.left()
    w3.arrived()
    for i in range(pieces):
        wgrad[i * rp : (i + 1) * rp, :] = wa_in[i]
    w3.left()


def hand_over(hidden, wgrad, fgrad, *rest):
    outs, sems = rest[:3], rest[3]
    copies = [
        pltpu.make_async_copy(src, dst, sems.at[i]) for i, (src, dst) in enumerate(zip((hidden, wgrad, fgrad), outs))
    ]
    for copy in copies:
        copy.start()
    for copy in copies:
        copy.wait()


class Sizes:
    def hops(self, offset):
        s, l, h, z = offset
        return min(s, self.ns - s) + l // 2 + 0.25 * (l % 2) + 2 * h + min(z, self.nz - z)


def on_device(feats, stale, weight, cot, send_sub, send_dom, tile_index, tile_count, tiles):
    c = Sizes()
    c.rows, f = feats.shape
    c.slots, c.tile = tiles.shape[0], tiles.shape[1]
    c.rb = c.rows // c.tile
    c.ns, c.ssub = send_sub.shape
    nd, c.sdom = send_dom.shape
    c.ng = 16 // c.sdom
    c.nz = nd // c.ng
    halo = c.ns * c.ssub + nd * c.sdom
    c.nh = -(-halo // c.tile)
    c.cb = c.rb + c.nh
    c.gpad = -(-c.nz * c.sdom // 16) * 16
    c.step = max(1, c.rb // 2)
    c.scale = float(1.0 / (c.rows * nd * c.ns) ** 0.5)
    hid = weight.shape[1]
    sub_total, dom_total = c.ns * c.ssub, nd * c.sdom
    c.nl = max(1, c.ng // 2)
    pieces, rest = c.ns * c.nl, c.ng // c.nl * c.nz
    rp = f // pieces
    vmem = pl.BlockSpec(memory_space=pltpu.VMEM)
    hbm = pl.BlockSpec(memory_space=pltpu.HBM)
    scratch = [
        pltpu.VMEM((c.rows, f), BF),
        pltpu.VMEM((c.cb, c.tile, f), BF),
        pltpu.VMEM((c.slots, c.tile, c.tile), BF),
        pltpu.VMEM((c.rows, hid), BF),
        pltpu.VMEM((c.slots, c.tile, f), F32),
        pltpu.VMEM((c.rb, c.tile, f), BF),
        pltpu.VMEM((c.rows, f), BF),
        pltpu.VMEM((c.rows, hid), BF),
        pltpu.VMEM((sub_total + c.ng * c.gpad, c.rows), BF),
        pltpu.VMEM((c.rows, sub_total), BF),
        pltpu.VMEM((c.rows, dom_total), BF),
        pltpu.VMEM((c.ns, c.ssub, f), BF),
        pltpu.VMEM((c.ng, c.gpad, f), BF),
        pltpu.VMEM((c.ng, c.gpad, f), BF),
        pltpu.VMEM((c.nz, c.ng * c.sdom, f), BF),
        pltpu.VMEM((c.nh * c.tile, f), BF),
        pltpu.VMEM((c.ns, c.ssub, f), BF),
        pltpu.VMEM((c.nz, c.ng * c.sdom, f), BF),
        pltpu.VMEM((c.ng, c.gpad, f), BF),
        pltpu.VMEM((c.ng, c.gpad, f), BF),
        pltpu.VMEM((dom_total, f), BF),
        pltpu.VMEM((pieces, rp, hid), F32),
        pltpu.VMEM((pieces, rp, hid), F32),
        pltpu.VMEM((rp, hid), F32),
        pltpu.VMEM((rest, rp, hid), F32),
        pltpu.VMEM((rp, hid), F32),
        pltpu.VMEM((pieces, rp, hid), F32),
        pltpu.VMEM((c.rows, f), F32),
        pltpu.VMEM((8, 128), I32),
        pltpu.SMEM((8, 128), I32),
        pltpu.VMEM((f, hid), BF),
        pltpu.VMEM((c.ns, c.ssub), I32),
        pltpu.VMEM((c.sdom, nd), I32),
        pltpu.VMEM((1, 2, c.slots), I32),
        pltpu.SMEM((1,), I32),
        pltpu.SemaphoreType.DMA((10,)),
        pltpu.SemaphoreType.DMA((9,)),
        pltpu.SemaphoreType.DMA((9,)),
    ]
    outs = (
        jax.ShapeDtypeStruct((c.rows, hid), BF),
        jax.ShapeDtypeStruct((f, hid), F32),
        jax.ShapeDtypeStruct((c.rows, f), BF),
    )
    results = pl.pallas_call(
        functools.partial(kernel, c),
        out_shape=tuple(pltpu.VMEM(o.shape, o.dtype) for o in outs),
        in_specs=[hbm] * 9,
        out_specs=(vmem, vmem, vmem),
        scratch_shapes=scratch,
        compiler_params=pltpu.CompilerParams(
            collective_id=0, has_side_effects=True, vmem_limit_bytes=62500 * 1024
        ),
    )(feats.reshape(c.rb, c.tile, f), stale, weight, cot, send_sub, send_dom.T, tile_index, tile_count, tiles)
    return pl.pallas_call(
        hand_over,
        out_shape=outs,
        in_specs=[vmem] * 3,
        out_specs=(hbm,) * 3,
        scratch_shapes=[pltpu.SemaphoreType.DMA((3,))],
        compiler_params=pltpu.CompilerParams(vmem_limit_bytes=2 * 1024 * 1024),
    )(*results)


def solution(mesh):
    rows = P(("dom", "sub"), None)
    cube = P(("dom", "sub"), None, None)
    return jax.shard_map(
        on_device,
        mesh=mesh,
        in_specs=(rows, rows, P(), rows, rows, rows, cube, P(("dom", "sub")), cube),
        out_specs=(rows, P(), rows),
        check_vma=False,
    )
```

```python
import functools

import jax
import jax.numpy as jnp
from jax import lax
from jax.experimental import pallas as pl
from jax.experimental.pallas import tpu as pltpu
from jax.sharding import PartitionSpec as P

BF = jnp.bfloat16
F32 = jnp.float32
I32 = jnp.int32
MESH = pl.DeviceIdType.MESH


def iota(shape, dim):
    return lax.broadcasted_iota(I32, shape, dim)


def dot(a, b):
    return jnp.dot(a, b, preferred_element_type=F32)


def dot_tn(a, b):
    return lax.dot_general(a, b, (((0,), (0,)), ((), ())), preferred_element_type=F32)


def dot_nt(a, b):
    return lax.dot_general(a, b, (((1,), (1,)), ((), ())), preferred_element_type=F32)


def one_hot(hit):
    return hit.astype(F32).astype(BF)


def slot_order(t, rb, nh):
    return jnp.where(t < nh, t + rb, jnp.where(t < nh + rb, t - nh, t))


def wrap(i, n):
    return jnp.where(i >= n, i - n, i)


def slot_chains(rb, nh, slots, tile_index, tile_count, out):
    out[...] = jnp.zeros_like(out)
    out[0:2, 0:slots] = tile_index[0]
    lanes = out.shape[1]
    count = tile_count[0]
    picks = out[...]
    u = iota((lanes, lanes), 0)
    t = iota((lanes, lanes), 1)
    ord_u = slot_order(u, rb, nh)
    ord_t = slot_order(t, rb, nh)
    for which in range(2):
        line = jnp.broadcast_to(picks[which : which + 1, :], (lanes, lanes))
        turned = line.T
        prev = jnp.where((turned == line) & (ord_u < ord_t) & (u < slots), ord_u, 0)
        last = jnp.where((turned == t) & (u < count), ord_u, 0)
        out[2 + 2 * which : 3 + 2 * which, :] = jnp.max(prev, axis=0, keepdims=True)
        out[3 + 2 * which : 4 + 2 * which, :] = jnp.max(last, axis=0, keepdims=True)


def total(terms):
    while len(terms) > 1:
        terms = [a + b for a, b in zip(terms[::2], terms[1::2])] + terms[len(terms) // 2 * 2 :]
    return terms[0]


class Exchange:
    def __init__(self, group, src, dst, block, ss, rs):
        self.copies = [
            pltpu.make_async_remote_copy(
                src_ref=src(peer), dst_ref=dst, send_sem=ss, recv_sem=rs, device_id=device, device_id_type=MESH
            )
            for peer, device in group
        ]
        self.block, self.ss, self.rs = block, ss, rs

    def start(self):
        for copy in self.copies:
            copy.start()

    def arrived(self):
        pltpu.make_async_copy(self.block, self.block, self.rs).wait()

    def left(self):
        pltpu.make_async_copy(self.block, self.block, self.ss).wait()


def kernel(
    c,
    feats, stale, weight_hbm, cot, sub_hbm, dom_hbm, index_hbm, count_hbm, tiles_hbm,
    hidden, wgrad, fgrad,
    st, xcols, tiles, cotv, chain, gbuf, aggv, gzv,
    ohg, ohs, ohd, sub_out, g_out, g_in, z_out, back, rsub, rz, rg_out, rg_in, rdom,
    wp_out, wp_in, wm_out, wm_in, wa_out, wa_in, acc,
    meta_v, meta_s, weight, send_sub, send_dom, tile_index, tile_count, sem_in, ss, rs,
):
    ns, ng, nz, tile, rb, nh, slots = c.ns, c.ng, c.nz, c.tile, c.rb, c.nh, c.slots
    rows, cb, ssub, sdom = c.rows, c.cb, c.ssub, c.sdom
    sub_total, dom_total = ns * ssub, ng * nz * sdom
    nd = ng * nz
    gpad, nl = c.gpad, c.nl
    d = lax.axis_index("dom")
    me_s = lax.axis_index("sub")
    me_z, me_g = d // ng, d % ng
    me_h, me_l = me_g // nl, me_g % nl

    stale_cp = pltpu.make_async_copy(stale, st, sem_in.at[0])
    feats_cp = pltpu.make_async_copy(feats, xcols.at[pl.ds(0, rb)], sem_in.at[1])
    tiles_cp = pltpu.make_async_copy(tiles_hbm, tiles, sem_in.at[2])
    cot_cp = pltpu.make_async_copy(cot, cotv, sem_in.at[3])
    dom_cp = pltpu.make_async_copy(dom_hbm, send_dom, sem_in.at[5])
    sub_cp = pltpu.make_async_copy(sub_hbm, send_sub, sem_in.at[6])
    index_cp = pltpu.make_async_copy(index_hbm, tile_index, sem_in.at[7])
    count_cp = pltpu.make_async_copy(count_hbm, tile_count, sem_in.at[8])
    weight_cp = pltpu.make_async_copy(weight_hbm, weight, sem_in.at[9])
    dom_cp.start()
    stale_cp.start()
    sub_cp.start()
    index_cp.start()
    count_cp.start()
    weight_cp.start()
    feats_cp.start()
    tiles_cp.start()
    cot_cp.start()

    def along(*steps):
        sizes = (ns, nl, ng // nl, nz)
        mine = (me_s, me_l, me_h, me_z)
        offsets = [()]
        for axis in range(4):
            offsets = [o + (k,) for o in offsets for k in range(sizes[axis] if axis in steps else 1)]
        offsets = sorted(offsets[1:], key=lambda o: -c.hops(o))
        group = []
        for offset in offsets:
            at = [wrap(m + o, n) if o else m for m, o, n in zip(mine, offset, sizes)]
            index = 0
            for axis in reversed(range(4)):
                if axis in steps:
                    index = index * sizes[axis] + at[axis]
            s, l, h, z = at
            group.append((index, {"dom": (z * (ng // nl) + h) * nl + l, "sub": s}))
        return group

    by_sub, by_g, by_z = along(0), along(1, 2), along(3)
    by_piece, by_rest = along(0, 1), along(2, 3)
    barrier = pltpu.get_barrier_semaphore()
    for _, device in (*by_g, *by_z, *by_sub):
        pl.semaphore_signal(barrier, inc=1, device_id=device, device_id_type=MESH)

    lane_n = iota((1, rows), 1)
    dom_cp.wait()
    dom_t = send_dom[...]
    dom_line = jnp.concatenate([dom_t[k : k + 1, :] for k in range(sdom)], axis=1)
    out_r = iota((ng * gpad, dom_total), 0)
    in_r = iota((ng * gpad, dom_total), 1)
    og, ozk = out_r // gpad, out_r % gpad
    want = (ozk % sdom) * nd + (ozk // sdom) * ng + og
    hit = (want == in_r) & (ozk < nz * sdom)
    dom_at = jnp.sum(jnp.where(hit, dom_line.astype(F32), 0.0), axis=1, keepdims=True)
    ohg[sub_total:, :] = one_hot(dom_at == lane_n.astype(F32))
    stale_cp.wait()
    g_out[...] = dot(ohg[sub_total:, :], st[...]).astype(BF).reshape(g_out.shape)
    pl.semaphore_wait(barrier, ns + ng + nz - 3)
    fg = Exchange(by_g, lambda p: g_out.at[p], g_in.at[me_g], g_in.at[pl.ds(0, ng - 1)], ss.at[0], rs.at[0])
    fg.start()
    g_in[pl.ds(me_g, 1)] = g_out[pl.ds(me_g, 1)]

    sub_cp.wait()
    sub_t = jnp.transpose(jnp.concatenate([send_sub[...], jnp.zeros((ns, 128 - ssub), I32)], axis=1))
    for j in range(ns):
        ohg[j * ssub : (j + 1) * ssub, :] = one_hot(sub_t[:ssub, j : j + 1] == lane_n)
    sub_out[...] = dot(ohg[0:sub_total, :], st[...]).astype(BF).reshape(sub_out.shape)
    per = tile // ssub
    sub_at = xcols.at[rb + me_s // per, pl.ds(pl.multiple_of(me_s % per * ssub, 16), ssub)]
    fs = Exchange(by_sub, lambda p: sub_out.at[p], sub_at, sub_out.at[pl.ds(0, ns - 1)], ss.at[1], rs.at[1])
    fs.start()
    sub_at[...] = sub_out[me_s]
    spare = (sub_total + dom_total) % tile
    if spare:
        xcols[cb - 1, spare:, :] = jnp.zeros((tile - spare, xcols.shape[2]), BF)

    index_cp.wait()
    count_cp.wait()
    slot_chains(rb, nh, slots, tile_index, tile_count, meta_v)
    meta_cp = pltpu.make_async_copy(meta_v, meta_s, sem_in.at[4])
    meta_cp.start()

    out_r = iota((dom_total, ng * gpad), 0)
    in_r = iota((dom_total, ng * gpad), 1)
    oz, ogk = out_r // (ng * sdom), out_r % (ng * sdom)
    want = (ogk // sdom) * gpad + oz * sdom + ogk % sdom
    turn_z = one_hot(want == in_r)
    fg.arrived()
    z_out[...] = dot(turn_z, g_in[...].reshape(ng * gpad, -1)).astype(BF).reshape(z_out.shape)
    zrows = ng * sdom
    z_row = sub_total + me_z * zrows
    z_at = xcols.at[rb + z_row // tile, pl.ds(pl.multiple_of(z_row % tile, 16), zrows)]
    fz = Exchange(by_z, lambda p: z_out.at[p], z_at, z_out.at[pl.ds(0, nz - 1)], ss.at[2], rs.at[2])
    fz.start()
    z_at[...] = z_out[me_z]

    feats_cp.wait()
    tiles_cp.wait()
    for p in range(rb):
        chain[p] = dot(tiles[nh + p], xcols[p])
    cot_cp.wait()
    weight_cp.wait()
    node = iota((rows, 1), 0)
    for j in range(sub_total // 128):
        pieces = [send_sub[i : i + 1, :] for i in range(j * 128 // ssub, (j + 1) * 128 // ssub)]
        ohs[:, j * 128 : (j + 1) * 128] = one_hot(jnp.concatenate(pieces, axis=1) == node)
    ohd[...] = one_hot(dom_line == node)
    meta_cp.wait()
    fs.arrived()

    for s in (*range(nh), *range(nh + rb, slots)):
        if s == sub_total // tile:
            fz.arrived()
        p = s + rb if s < nh else s
        block = xcols[rb + s] if s < nh else xcols[meta_s[1, s]]
        chain[p] = dot(tiles[s], block) + chain[meta_s[2, s]]

    step = c.step
    w = weight[...]
    for b in range(rb // step):
        lo, hi = b * step * tile, (b + 1) * step * tile
        for r in range(b * step, (b + 1) * step):
            aggv[r * tile : (r + 1) * tile, :] = chain[meta_s[3, r]].astype(BF)
        agg = aggv[lo:hi, :]
        pre = dot(agg, w)
        sig = jax.nn.sigmoid(pre)
        gz = (cotv[lo:hi, :].astype(F32) * sig * (1.0 + pre * (1.0 - sig))).astype(BF)
        gzv[lo:hi, :] = gz
    part = dot_tn(aggv[...], gzv[...])
    pieces = wp_out.shape[0]
    rp = wp_out.shape[1]
    for i in range(pieces):
        wp_out[i] = part[i * rp : (i + 1) * rp, :]

    me_p = me_l * ns + me_s
    w1 = Exchange(by_piece, lambda p: wp_out.at[p], wp_in.at[me_p], wp_in.at[pl.ds(0, pieces - 1)], ss.at[3], rs.at[3])
    w1.start()
    wp_in[pl.ds(me_p, 1)] = wp_out[pl.ds(me_p, 1)]

    for b in range(rb // step):
        gz = gzv[b * step * tile : (b + 1) * step * tile, :]
        gbuf[b * step : (b + 1) * step] = dot_nt(gz, w).astype(BF).reshape(step, tile, -1)
    for s in range(slots):
        p = s + rb if s < nh else (s - nh if s < nh + rb else s)
        block = gbuf[s - nh] if nh <= s < nh + rb else gbuf[meta_s[0, s]]
        term = dot_tn(tiles[s], block)
        chain[p] = term if p < cb else term + chain[meta_s[4, s]]
    for h in range(nh):
        back[h * tile : (h + 1) * tile, :] = chain[meta_s[5, rb + h]].astype(BF)

    def back_z(p):
        return back.at[pl.ds(pl.multiple_of(sub_total + p * zrows, 16), zrows)]

    def back_s(p):
        return back.at[pl.ds(pl.multiple_of(p * ssub, 16), ssub)]

    bz = Exchange(by_z, back_z, rz.at[me_z], rz.at[pl.ds(0, nz - 1)], ss.at[4], rs.at[4])
    bz.start()
    bs = Exchange(by_sub, back_s, rsub.at[me_s], rsub.at[pl.ds(0, ns - 1)], ss.at[5], rs.at[5])
    bs.start()
    rz[pl.ds(me_z, 1)] = back_z(me_z)[...].reshape(1, zrows, -1)
    rsub[pl.ds(me_s, 1)] = back_s(me_s)[...].reshape(1, ssub, -1)
    out_r = iota((ng * gpad, dom_total), 0)
    in_r = iota((ng * gpad, dom_total), 1)
    og, ozk = out_r // gpad, out_r % gpad
    want = (ozk // sdom) * zrows + og * sdom + ozk % sdom
    turn_g = one_hot((want == in_r) & (ozk < nz * sdom))

    w1.arrived()
    piece = total([wp_in[i] for i in range(pieces)])
    wm_out[...] = piece
    rest = wm_in.shape[0]
    me_r = me_z * (ng // nl) + me_h
    w2 = Exchange(by_rest, lambda p: wm_out, wm_in.at[me_r], wm_in.at[pl.ds(0, rest - 1)], ss.at[6], rs.at[6])
    w2.start()
    wm_in[pl.ds(me_r, 1)] = piece[None]

    bz.arrived()
    rg_out[...] = dot(turn_g, rz[...].reshape(dom_total, -1)).astype(BF).reshape(rg_out.shape)
    bg = Exchange(by_g, lambda p: rg_out.at[p], rg_in.at[me_g], rg_in.at[pl.ds(0, ng - 1)], ss.at[7], rs.at[7])
    bg.start()
    rg_in[pl.ds(me_g, 1)] = rg_out[pl.ds(me_g, 1)]

    for b in range(rb // step):
        lo, hi = b * step * tile, (b + 1) * step * tile
        pre = dot(aggv[lo:hi, :], w)
        hidden[lo:hi, :] = (pre * jax.nn.sigmoid(pre)).astype(BF)

    bs.arrived()
    for b in range(rb // step):
        lo, hi = b * step * tile, (b + 1) * step * tile
        got = dot(ohs[lo:hi, :], rsub[...].reshape(sub_total, -1))
        for r in range(step):
            acc[lo + r * tile : lo + (r + 1) * tile, :] = chain[meta_s[5, b * step + r]] + got[r * tile : (r + 1) * tile, :]

    w2.arrived()
    piece = total([wm_in[i] for i in range(rest)]) * c.scale
    wa_out[...] = piece
    w3 = Exchange(by_piece, lambda p: wa_out, wa_in.at[me_p], wa_in.at[pl.ds(0, pieces - 1)], ss.at[8], rs.at[8])
    w3.start()
    wa_in[pl.ds(me_p, 1)] = piece[None]

    out_r = iota((dom_total, ng * gpad), 0)
    in_r = iota((dom_total, ng * gpad), 1)
    ok, ozg = out_r // nd, out_r % nd
    want = (ozg % ng) * gpad + (ozg // ng) * sdom + ok
    turn_k = one_hot(want == in_r)
    bg.arrived()
    rdom[...] = dot(turn_k, rg_in[...].reshape(ng * gpad, -1)).astype(BF)
    for b in range(rb // step):
        lo, hi = b * step * tile, (b + 1) * step * tile
        fgrad[lo:hi, :] = (acc[lo:hi, :] + dot(ohd[lo:hi, :], rdom[...])).astype(BF)

    for x in (fg, fs, fz, bz, bs, bg, w1, w2):
        x.left()
    w3.arrived()
    for i in range(pieces):
        wgrad[i * rp : (i + 1) * rp, :] = wa_in[i]
    w3.left()


def hand_over(hidden, wgrad, fgrad, *rest):
    outs, sems = rest[:3], rest[3]
    copies = [
        pltpu.make_async_copy(src, dst, sems.at[i]) for i, (src, dst) in enumerate(zip((hidden, wgrad, fgrad), outs))
    ]
    for copy in copies:
        copy.start()
    for copy in copies:
        copy.wait()


class Sizes:
    def hops(self, offset):
        s, l, h, z = offset
        return min(s, self.ns - s) + l // 2 + 0.25 * (l % 2) + 2 * h + min(z, self.nz - z)


def on_device(feats, stale, weight, cot, send_sub, send_dom, tile_index, tile_count, tiles):
    c = Sizes()
    c.rows, f = feats.shape
    c.slots, c.tile = tiles.shape[0], tiles.shape[1]
    c.rb = c.rows // c.tile
    c.ns, c.ssub = send_sub.shape
    nd, c.sdom = send_dom.shape
    c.ng = 16 // c.sdom
    c.nz = nd // c.ng
    halo = c.ns * c.ssub + nd * c.sdom
    c.nh = -(-halo // c.tile)
    c.cb = c.rb + c.nh
    c.gpad = -(-c.nz * c.sdom // 16) * 16
    c.step = c.rb
    c.scale = float(1.0 / (c.rows * nd * c.ns) ** 0.5)
    hid = weight.shape[1]
    sub_total, dom_total = c.ns * c.ssub, nd * c.sdom
    c.nl = max(1, c.ng // 2)
    pieces, rest = c.ns * c.nl, c.ng // c.nl * c.nz
    rp = f // pieces
    vmem = pl.BlockSpec(memory_space=pltpu.VMEM)
    hbm = pl.BlockSpec(memory_space=pltpu.HBM)
    scratch = [
        pltpu.VMEM((c.rows, f), BF),
        pltpu.VMEM((c.cb, c.tile, f), BF),
        pltpu.VMEM((c.slots, c.tile, c.tile), BF),
        pltpu.VMEM((c.rows, hid), BF),
        pltpu.VMEM((c.slots, c.tile, f), F32),
        pltpu.VMEM((c.rb, c.tile, f), BF),
        pltpu.VMEM((c.rows, f), BF),
        pltpu.VMEM((c.rows, hid), BF),
        pltpu.VMEM((sub_total + c.ng * c.gpad, c.rows), BF),
        pltpu.VMEM((c.rows, sub_total), BF),
        pltpu.VMEM((c.rows, dom_total), BF),
        pltpu.VMEM((c.ns, c.ssub, f), BF),
        pltpu.VMEM((c.ng, c.gpad, f), BF),
        pltpu.VMEM((c.ng, c.gpad, f), BF),
        pltpu.VMEM((c.nz, c.ng * c.sdom, f), BF),
        pltpu.VMEM((c.nh * c.tile, f), BF),
        pltpu.VMEM((c.ns, c.ssub, f), BF),
        pltpu.VMEM((c.nz, c.ng * c.sdom, f), BF),
        pltpu.VMEM((c.ng, c.gpad, f), BF),
        pltpu.VMEM((c.ng, c.gpad, f), BF),
        pltpu.VMEM((dom_total, f), BF),
        pltpu.VMEM((pieces, rp, hid), F32),
        pltpu.VMEM((pieces, rp, hid), F32),
        pltpu.VMEM((rp, hid), F32),
        pltpu.VMEM((rest, rp, hid), F32),
        pltpu.VMEM((rp, hid), F32),
        pltpu.VMEM((pieces, rp, hid), F32),
        pltpu.VMEM((c.rows, f), F32),
        pltpu.VMEM((8, 128), I32),
        pltpu.SMEM((8, 128), I32),
        pltpu.VMEM((f, hid), BF),
        pltpu.VMEM((c.ns, c.ssub), I32),
        pltpu.VMEM((c.sdom, nd), I32),
        pltpu.VMEM((1, 2, c.slots), I32),
        pltpu.SMEM((1,), I32),
        pltpu.SemaphoreType.DMA((10,)),
        pltpu.SemaphoreType.DMA((9,)),
        pltpu.SemaphoreType.DMA((9,)),
    ]
    outs = (
        jax.ShapeDtypeStruct((c.rows, hid), BF),
        jax.ShapeDtypeStruct((f, hid), F32),
        jax.ShapeDtypeStruct((c.rows, f), BF),
    )
    results = pl.pallas_call(
        functools.partial(kernel, c),
        out_shape=tuple(pltpu.VMEM(o.shape, o.dtype) for o in outs),
        in_specs=[hbm] * 9,
        out_specs=(vmem, vmem, vmem),
        scratch_shapes=scratch,
        compiler_params=pltpu.CompilerParams(
            collective_id=0, has_side_effects=True, vmem_limit_bytes=62500 * 1024
        ),
    )(feats.reshape(c.rb, c.tile, f), stale, weight, cot, send_sub, send_dom.T, tile_index, tile_count, tiles)
    return pl.pallas_call(
        hand_over,
        out_shape=outs,
        in_specs=[vmem] * 3,
        out_specs=(hbm,) * 3,
        scratch_shapes=[pltpu.SemaphoreType.DMA((3,))],
        compiler_params=pltpu.CompilerParams(vmem_limit_bytes=2 * 1024 * 1024),
    )(*results)


def solution(mesh):
    rows = P(("dom", "sub"), None)
    cube = P(("dom", "sub"), None, None)
    return jax.shard_map(
        on_device,
        mesh=mesh,
        in_specs=(rows, rows, P(), rows, rows, rows, cube, P(("dom", "sub")), cube),
        out_specs=(rows, P(), rows),
        check_vma=False,
    )
```
